128 devices in a mesh: section: 2 (over core), dp: 32 (over z, y, x_hi), tensor: 2 (over x_lo).
Axes of the slice: x: 4 (x_hi: 2, x_lo: 2; x = x_hi * 2 + x_lo), y: 4, z: 4, core: 2. Of those that a mesh axis runs over, the one named last changes fastest.
Arguments:
- tokens: bfloat16 [32, 8, 48, 5120], P('dp', None, 'tensor'), may hold values from -6 to 6
- doc_ids: int32 [32, 384], P('dp'), may hold values from 0 to 3, never falling along the last dimension, each value on 1 to 192 neighbouring positions
- norm_gain: float32 [2, 5120], P('section'), may hold values from 0.1 to 1.9
- w_query: bfloat16 [2, 5120, 2560], P('section', 'dp', 'tensor'), may hold values from -0.078125 to 0.078125
- w_key: bfloat16 [2, 5120, 512], P('section', None, 'tensor'), may hold values from -0.078125 to 0.078125
- w_value: bfloat16 [2, 5120, 512], P('section', None, 'tensor'), may hold values from -0.078125 to 0.078125
- w_out: bfloat16 [2, 2560, 5120], P('section', 'tensor', 'dp'), may hold values from -0.125 to 0.125
Outputs:
- layer_states: bfloat16 [2, 32, 8, 48, 5120], P('section', 'dp', None, 'tensor')
The draws below stay inside these ranges and needn't reach their ends.
Inputs may be any that keep to these rules, and one draw needn't show every extreme that they name: `doc_ids`: each sequence's positions are cut into consecutive whole documents numbered from 0 in order, none longer than 192 positions, one exactly that long.
All inputs are finite; a program needn't handle non-finite values.
Results may differ from the reference program's by a relative error of at most 0.018.
Values may be sent and summed in bfloat16 or wider, within the bound.
A program may use at most 128 MiB of HBM per device.

```python
import math
import jax
import jax.numpy as jnp
import numpy as np
from jax import lax

D = 5120
HEADS = 20
KV_HEADS = 4
HEAD = 128
SEG = 48
NSEG = 8
DOCS = 4
LAYERS = 2
SEQ = 384
N_DP = 32
N_TENSOR = 2


def steps_of(own_key, shape, cuts, smallest, top_value):
    level, own = 1.0, jax.random.fold_in(own_key, 6)
    for axis_at, shards_of in cuts:
        heights = jnp.exp(jax.random.uniform(jax.random.fold_in(own, axis_at), (shards_of,), jnp.float32, smallest / len(cuts), top_value / len(cuts)))
        level = level * jnp.repeat(heights, shape[axis_at] // shards_of).reshape([-1 if axis == axis_at else 1 for axis in range(len(shape))])
    return level


def length_profile(amount, total, bound, skew):
    loads = [(1 << 20) // math.isqrt(standing ** skew) + 1 for standing in range(2, amount + 1)]
    spare, holding = total - bound - (amount - 1), [1] * (amount - 1)
    while spare > 0:
        movable = [i for i in range(amount - 1) if holding[i] < bound]
        mass, left = sum([loads[i] for i in movable]), spare
        for i in movable:
            addition = min(bound - holding[i], max(1, left * loads[i] // mass), spare)
            holding[i] = holding[i] + addition
            spare = spare - addition
    return np.array([bound] + holding)


def ragged_sizes(own_key, number_of, total, bound, lean):
    if number_of == 2:
        one = jax.random.randint(own_key, (), max(1, total - bound), min(bound, total - 1) + 1)
        return jnp.stack([one, total - one])
    tallies = jnp.asarray(length_profile(number_of, total, bound, lean), jnp.int32)
    twos = (number_of - 1) // 2
    donor, receiver = tallies[1:1 + 2 * twos:2], tallies[2:2 + 2 * twos:2]
    slack = jnp.minimum(donor - 1, bound - receiver)
    shifted = jax.random.randint(jax.random.fold_in(own_key, 1), (twos,), 0, 1 << 20) % (slack + 1)
    tallies = tallies.at[1:1 + 2 * twos:2].set(donor - shifted).at[2:2 + 2 * twos:2].set(receiver + shifted)
    return tallies[jax.random.permutation(jax.random.fold_in(own_key, 2), number_of)]


def normal_values(stream_key, shape, spread, most, split=(), kind=jnp.bfloat16):
    array = spread * jax.random.normal(stream_key, shape, jnp.float32)
    if split:
        array = array * steps_of(stream_key, shape, split, -0.22, 0.18)
    return jnp.clip(array, -most, most).astype(kind)


def setup_inputs(seed: int = 0) -> dict:
    seeds = jax.random.split(jax.random.key(seed), 8)
    tokens = normal_values(seeds[0], (N_DP, NSEG, SEG, D), 1.0, 6.0, ((0, 32), (2, 2)))
    doc_ids = jax.vmap(lambda own: jnp.searchsorted(jnp.cumsum(ragged_sizes(own, DOCS, SEQ, SEQ // 2, 0)), jnp.arange(SEQ), side="right"))(jax.random.split(seeds[1], N_DP)).reshape((N_DP, SEQ)).astype(jnp.int32)
    norm_gain = jnp.clip(1.0 + 0.18 * jax.random.normal(seeds[2], (LAYERS, D), jnp.float32), 0.1, 1.9)
    w_query = normal_values(seeds[3], (LAYERS, D, HEADS * HEAD), D ** -0.5, 0.078125, ((0, 2), (1, 32), (2, 2)))
    w_key = normal_values(seeds[4], (LAYERS, D, KV_HEADS * HEAD), D ** -0.5, 0.078125, ((0, 2), (2, 2)))
    w_value = normal_values(seeds[5], (LAYERS, D, KV_HEADS * HEAD), D ** -0.5, 0.078125, ((0, 2), (2, 2)))
    w_out = normal_values(seeds[6], (LAYERS, HEADS * HEAD, D), (HEADS * HEAD) ** -0.5, 0.125, ((0, 2), (1, 2), (2, 32)))
    return {"tokens": tokens, "doc_ids": doc_ids, "norm_gain": norm_gain, "w_query": w_query, "w_key": w_key, "w_value": w_value, "w_out": w_out}


def one_layer(hidden, gain, w_q, w_k, w_v, w_o, docs):
    batch = hidden.shape[0]
    group = HEADS // KV_HEADS
    wide = hidden.astype(jnp.float32)
    normed = (wide * lax.rsqrt(lax.optimization_barrier(jnp.mean(wide * wide, axis=-1, keepdims=True)) + 1e-06) * gain).astype(jnp.bfloat16)
    flat = normed.reshape(batch * SEQ, D)
    query = jnp.dot(flat, w_q, preferred_element_type=jnp.float32).astype(jnp.bfloat16)
    key = jnp.dot(flat, w_k, preferred_element_type=jnp.float32).astype(jnp.bfloat16)
    value = jnp.dot(flat, w_v, preferred_element_type=jnp.float32).astype(jnp.bfloat16)
    query = query.reshape(batch, SEQ, KV_HEADS, group, HEAD).astype(jnp.float32)
    key = key.reshape(batch, SEQ, KV_HEADS, HEAD).astype(jnp.float32)
    value = value.reshape(batch, SEQ, KV_HEADS, HEAD).astype(jnp.float32)
    scores = jnp.einsum('bqkgd,bskd->bkgqs', query, key) * (1.0 / HEAD ** 0.5)
    place = jnp.arange(SEQ, dtype=jnp.int32)
    allowed = (place[None, :] <= place[:, None])[None] & (docs[:, None, :] == docs[:, :, None])
    scores = jnp.where(allowed[:, None, None], scores, -1e+30)
    weights = jax.nn.softmax(scores, axis=-1).astype(jnp.bfloat16)
    attended = jnp.einsum('bkgqs,bskd->bqkgd', weights.astype(jnp.float32), value).astype(jnp.bfloat16)
    attended = attended.reshape(batch * SEQ, N_TENSOR, HEADS * HEAD // N_TENSOR)
    out_groups = w_o.reshape(N_TENSOR, HEADS * HEAD // N_TENSOR, D)
    update = jnp.zeros((batch * SEQ, D), jnp.float32)
    for part in range(N_TENSOR):
        term = jnp.dot(attended[:, part], out_groups[part], preferred_element_type=jnp.float32).astype(jnp.bfloat16)
        update = update + lax.optimization_barrier(term).astype(jnp.float32)
    return (wide + update.reshape(batch, SEQ, D)).astype(jnp.bfloat16)

def reference(tokens, doc_ids, norm_gain, w_query, w_key, w_value, w_out):
    batch = tokens.shape[0]
    hidden = tokens.reshape(batch, SEQ, D)
    states = []
    for layer in range(LAYERS):
        hidden = one_layer(hidden, norm_gain[layer], w_query[layer], w_key[layer], w_value[layer], w_out[layer], doc_ids)
        states.append(hidden.reshape(batch, NSEG, SEG, D))
    return jnp.stack(states)
```

```python
import functools

import jax
import jax.numpy as jnp
from jax import lax
from jax.experimental import pallas as pl
from jax.experimental.pallas import tpu as pltpu
from jax.sharding import PartitionSpec as P

HEAD = 128
MESH = pl.DeviceIdType.MESH
RING = 4
PARTS = 8
ORDER = (0, 3, 1, 2)


def layer_kernel(
    tok, docs_col, docs_row, pos_col, pos_row, gain, wq, wot, wk, wv, out,
    full_q, full_o, kv_w, hidden, normed, query, key, value, attended, bias, part, part_in, fresh,
    w_recv, w_send, x_recv, x_send, own_sem, kv_sem, h_sem, h_send, p_recv, p_send, n_send, o_sem, gate,
):
    section = lax.axis_index("section")
    dp = lax.axis_index("dp")
    tensor = lax.axis_index("tensor")
    z, y, far = dp // 8, (dp // 2) % RING, dp % 2
    rows = tok.shape[0]
    seq = 2 * rows
    width = tok.shape[1]
    block = wq.shape[0]
    half = block // 2
    q_width = wq.shape[1]
    chunk = width // PARTS
    weights = (full_q, full_o)
    shards = (wq, wot)

    def at(dz, dy):
        return (section, ((z + dz) % RING) * 8 + ((y + dy) % RING) * 2 + far, tensor)

    opposite = (section, z * 8 + y * 2 + (1 - far), tensor)
    partner = (section, dp, 1 - tensor)
    core = (1 - section, dp, tensor)
    partner_core = (1 - section, dp, 1 - tensor)
    peers = [at(1, 0), at(-1, 0), at(0, 1), at(0, -1), opposite, partner, core, partner_core]
    barrier = pltpu.get_barrier_semaphore()
    for peer in peers:
        pl.semaphore_signal(barrier, inc=1, device_id=peer, device_id_type=MESH)

    def zy(cls, fo, go):
        return (fo, go) if cls == 0 else (go, fo)

    def piece(w, cls, fo, go, h):
        dz, dy = zy(cls, fo, go)
        first = (((z + dz) % RING) * 8 + ((y + dy) % RING) * 2 + cls) * block + h * half
        return weights[w].at[pl.ds(pl.multiple_of(first, 16), half), :]

    def own_piece(w, which, h):
        first = (z * 8 + y * 2 + which) * block + h * half
        return weights[w].at[pl.ds(pl.multiple_of(first, 16), half), :]

    def send_of(w, cls, fo, go, h, along_f, step):
        src = piece(w, cls, fo, go, h)
        to_fo = (fo - step) % RING if along_f else fo
        to_go = go if along_f else (go - step) % RING
        dz, dy = zy(cls, step, 0) if along_f else zy(cls, 0, step)
        return pltpu.make_async_remote_copy(
            src_ref=src,
            dst_ref=src,
            send_sem=w_send.at[w, cls, to_fo * 4 + to_go, h],
            recv_sem=w_recv.at[w, cls, to_fo * 4 + to_go, h],
            device_id=at(dz, dy),
            device_id_type=MESH,
        )

    def wait_piece(w, cls, fo, go, h):
        ref = piece(w, cls, fo, go, h)
        pltpu.make_async_remote_copy(
            src_ref=ref, dst_ref=ref, send_sem=w_send.at[w, cls, fo * 4 + go, h],
            recv_sem=w_recv.at[w, cls, fo * 4 + go, h], device_id=at(1, 0), device_id_type=MESH,
        ).wait_recv()

    sends = []

    def send(*which):
        copy = send_of(*which)
        copy.start()
        sends.append(which)

    def across(w, h):
        return pltpu.make_async_remote_copy(
            src_ref=shards[w].at[pl.ds(h * half, half), :], dst_ref=own_piece(w, far, h),
            send_sem=x_send.at[w, h], recv_sem=x_recv.at[w, h], device_id=opposite, device_id_type=MESH,
        )

    def across_in(w, h):
        ref = own_piece(w, 1 - far, h)
        pltpu.make_async_remote_copy(
            src_ref=ref, dst_ref=ref, send_sem=x_send.at[w, h], recv_sem=x_recv.at[w, h],
            device_id=opposite, device_id_type=MESH,
        ).wait_recv()

    def own_copy(w, h):
        return pltpu.make_async_copy(
            shards[w].at[pl.ds(h * half, half), :], own_piece(w, far, h), own_sem.at[w, h]
        )

    def first_sends(w, cls, log):
        for h in (0, 1):
            for along_f in (True, False):
                for step in ((1, -1) if h == 0 else (-1, 1)):
                    which = (w, cls, 0, 0, h, along_f, step)
                    send_of(*which).start()
                    if log:
                        sends.append(which)

    def open_gather(w):
        for cls in (0, 1):
            for h in (0, 1):
                for along_f in (True, False):
                    for step in (1, -1):
                        sends.append((w, cls, 0, 0, h, along_f, step))
        for mine in (0, 1):

            @pl.when(far == mine)
            def _():
                for h in (0, 1):
                    own_copy(w, h).wait()
                first_sends(w, mine, False)
                for h in (0, 1):
                    across_in(w, h)
                first_sends(w, 1 - mine, False)

    def spread(w, cls, fo, h):
        def event():
            wait_piece(w, cls, fo, 0, h)
            if fo == 3 and h == 0:
                send(w, cls, fo, 0, h, True, 1)
            if fo == 1 and h == 1:
                send(w, cls, fo, 0, h, True, -1)
            send(w, cls, fo, 0, h, False, 1)
            send(w, cls, fo, 0, h, False, -1)

        return event

    def relay(w, cls, fo, go):
        def event():
            h = 0 if go == 3 else 1
            wait_piece(w, cls, fo, go, h)
            send(w, cls, fo, go, h, False, 1 if go == 3 else -1)

        return event

    def events_of(w):
        early, late = [], []
        for fo, h in ((3, 0), (1, 1), (3, 1), (1, 0), (2, 0), (2, 1)):
            for cls in (0, 1):
                early.append(spread(w, cls, fo, h))
        for fo in ORDER:
            for cls in (0, 1):
                for go in (3, 1):
                    late.append(relay(w, cls, fo, go))
        return early, late

    def rest_of(w, cls, fo, go):
        for h in (0, 1):
            if not (go == 3 and h == 0) and not (go == 1 and h == 1):
                wait_piece(w, cls, fo, go, h)

    def rows_of(which):
        return pl.ds(pl.multiple_of(which * rows, 16), rows)

    def cols_of(k):
        first = ((z + ORDER[k // 2]) % RING) * (2 * chunk) + (k % 2) * chunk
        return pl.ds(pl.multiple_of(first, 128), chunk)

    kv_copies = [
        pltpu.make_async_copy(wk, kv_w.at[0], kv_sem.at[0]),
        pltpu.make_async_copy(wv, kv_w.at[1], kv_sem.at[1]),
    ]
    for h in (0, 1):
        own_copy(0, h).start()
    for h in (0, 1):
        own_copy(1, h).start()
    for copy in kv_copies:
        copy.start()
    pl.semaphore_wait(barrier, len(peers))
    for w in (0, 1):
        for h in (0, 1):
            across(w, h).start()

    def token_copy(k):
        return pltpu.make_async_copy(
            tok.at[:, cols_of(k)], hidden.at[rows_of(tensor), cols_of(k)], h_sem.at[0, k]
        )

    def token_send(k):
        return pltpu.make_async_remote_copy(
            src_ref=tok.at[:, cols_of(k)], dst_ref=hidden.at[rows_of(tensor), cols_of(k)],
            send_sem=h_send.at[k], recv_sem=h_sem.at[1, k], device_id=partner, device_id_type=MESH,
        )

    @pl.when(section == 0)
    def _():
        for k in range(PARTS):
            token_copy(k).start()
            token_send(k).start()

    @pl.when(section == 1)
    def _():
        pl.semaphore_wait(gate, 1)

    early_q, late_q = events_of(0)
    early_o, late_o = events_of(1)
    open_gather(0)
    for event in early_q:
        event()
    for event in late_q[:12]:
        event()
    open_gather(1)
    for event in late_q[12:]:
        event()

    allowed = (pos_row[...] <= pos_col[...]) & (docs_row[...] == docs_col[...])
    bias[...] = jnp.where(allowed, 0.0, -1e30)

    pending = early_o + late_o[:12]

    def pump(count):
        for _ in range(min(count, len(pending))):
            pending.pop(0)()

    pump(4)
    for k in range(PARTS):
        for src, whose in ((0, tensor), (1, 1 - tensor)):
            ref = hidden.at[rows_of(whose), cols_of(k)]
            pltpu.make_async_copy(ref, ref, h_sem.at[src, k]).wait()
    pump(2)

    step_rows = 16

    def normalise(i, _):
        place = pl.ds(pl.multiple_of(i * step_rows, step_rows), step_rows)
        wide = hidden[place, :].astype(jnp.float32)
        level = lax.rsqrt(jnp.mean(wide * wide, axis=-1, keepdims=True) + 1e-06)
        normed[place, :] = (wide * level * gain[...]).astype(jnp.bfloat16)
        return 0

    lax.fori_loop(0, seq // step_rows, normalise, 0)
    pump(3)
    for copy in kv_copies:
        copy.wait()
    key[...] = jnp.dot(normed[...], kv_w[0], preferred_element_type=jnp.float32).astype(jnp.bfloat16)
    value[...] = jnp.dot(normed[...], kv_w[1], preferred_element_type=jnp.float32).astype(jnp.bfloat16)
    pump(3)

    for cls in (0, 1):
        for fo in range(RING):
            for go in (3, 1, 2):
                rest_of(0, cls, fo, go)

    tile = 256

    def project(i, _):
        cols = pl.ds(pl.multiple_of(i * tile, tile), tile)
        query[:, cols] = jnp.dot(
            normed[...], full_q[:, cols], preferred_element_type=jnp.float32
        ).astype(jnp.bfloat16)
        return 0

    tiles = q_width // tile
    lax.fori_loop(0, 2, project, 0)
    pump(3)
    lax.fori_loop(2, tiles, project, 0)
    pump(3)

    scale = 1.0 / HEAD**0.5
    heads = q_width // HEAD
    group = heads // (key.shape[1] // HEAD)

    def attend(kv, h):
        cols = pl.ds(pl.multiple_of(h * HEAD, HEAD), HEAD)
        kv_cols = pl.ds(kv * HEAD, HEAD)
        scores = lax.dot_general(
            query[:, cols], key[:, kv_cols], (((1,), (1,)), ((), ())), preferred_element_type=jnp.float32
        )
        scores = scores * scale + bias[...]
        scores = jnp.exp(scores - jnp.max(scores, axis=-1, keepdims=True))
        mix = (scores / jnp.sum(scores, axis=-1, keepdims=True)).astype(jnp.bfloat16)
        attended[:, cols] = jnp.dot(
            mix, value[:, kv_cols], preferred_element_type=jnp.float32
        ).astype(jnp.bfloat16)

    for kv in range(heads // group):
        for lo, hi in ((0, 3), (3, group)):
            lax.fori_loop(kv * group + lo, kv * group + hi, lambda h, c, kv=kv: (attend(kv, h), c)[1], 0)
            pump(2)
    pump(len(pending))

    @pl.when(section == 0)
    def _():
        pl.semaphore_signal(gate, inc=1, device_id=core, device_id_type=MESH)

    def part_send(k):
        return pltpu.make_async_remote_copy(
            src_ref=part.at[k, rows_of(1 - tensor), :], dst_ref=part_in.at[k],
            send_sem=p_send.at[k], recv_sem=p_recv.at[k], device_id=partner, device_id_type=MESH,
        )

    def out_copy(k):
        return pltpu.make_async_copy(fresh.at[:, cols_of(k)], out.at[:, cols_of(k)], o_sem.at[k])

    def next_send(k, side):
        return pltpu.make_async_remote_copy(
            src_ref=fresh.at[:, cols_of(k)], dst_ref=hidden.at[rows_of(tensor), cols_of(k)],
            send_sem=n_send.at[side, k], recv_sem=h_sem.at[side, k],
            device_id=core if side == 0 else partner_core, device_id_type=MESH,
        )

    def finish(k):
        part_send(k).wait_recv()
        own = hidden[rows_of(tensor), cols_of(k)].astype(jnp.float32)
        update = part[k, rows_of(tensor), :].astype(jnp.float32) + part_in[k].astype(jnp.float32)
        fresh[:, cols_of(k)] = (own + update).astype(jnp.bfloat16)
        out_copy(k).start()

        @pl.when(section == 0)
        def _():
            next_send(k, 0).start()
            next_send(k, 1).start()

    for k in range(PARTS):
        if k % 2 == 0:
            slab = ORDER[k // 2]
            if slab == 3:
                for event in late_o[12:]:
                    event()
            if slab == 0:
                for fo in range(RING):
                    if fo:
                        pass
                for go in (3, 1, 2):
                    rest_of(1, 0, 0, go)
            else:
                for go in (3, 1, 2):
                    rest_of(1, 0, slab, go)
                for fo in range(RING):
                    rest_of(1, 1, fo, slab)
        result = lax.dot_general(
            attended[...], full_o[cols_of(k), :], (((1,), (1,)), ((), ())), preferred_element_type=jnp.float32
        )
        part[k] = result.astype(jnp.bfloat16)
        part_send(k).start()
        if k >= 2:
            finish(k - 2)
    finish(PARTS - 2)
    finish(PARTS - 1)

    for which in sends:
        send_of(*which).wait_send()
    for w in (0, 1):
        for h in (0, 1):
            across(w, h).wait_send()
    for k in range(PARTS):
        part_send(k).wait_send()
        out_copy(k).wait()

    @pl.when(section == 0)
    def _():
        for k in range(PARTS):
            token_send(k).wait_send()
            next_send(k, 0).wait_send()
            next_send(k, 1).wait_send()


def on_device(tokens, doc_ids, norm_gain, w_query, w_key, w_value, w_out):
    n_segments, quarter, width = tokens.shape[1:]
    rows = n_segments * quarter
    seq = 2 * rows
    block, q_width = w_query.shape[1:]
    kv_width = w_key.shape[2]
    chunk = width // PARTS
    docs = doc_ids[0].reshape(n_segments, 2, quarter).transpose(1, 0, 2).reshape(seq)
    pos = jnp.arange(seq, dtype=jnp.int32).reshape(n_segments, 2, quarter).transpose(1, 0, 2).reshape(seq)
    bf16 = jnp.bfloat16
    dma = pltpu.SemaphoreType.DMA
    anywhere = pl.BlockSpec(memory_space=pl.ANY)
    vmem = pl.BlockSpec(memory_space=pltpu.VMEM)
    state = pl.pallas_call(
        layer_kernel,
        out_shape=jax.ShapeDtypeStruct((rows, width), bf16),
        in_specs=[anywhere] + [vmem] * 5 + [anywhere] * 4,
        out_specs=anywhere,
        scratch_shapes=[
            pltpu.VMEM((width, q_width), bf16),
            pltpu.VMEM((width, q_width), bf16),
            pltpu.VMEM((2, width, kv_width), bf16),
            pltpu.VMEM((seq, width), bf16),
            pltpu.VMEM((seq, width), bf16),
            pltpu.VMEM((seq, q_width), bf16),
            pltpu.VMEM((seq, kv_width), bf16),
            pltpu.VMEM((seq, kv_width), bf16),
            pltpu.VMEM((seq, q_width), bf16),
            pltpu.VMEM((seq, seq), jnp.float32),
            pltpu.VMEM((PARTS, seq, chunk), bf16),
            pltpu.VMEM((PARTS, rows, chunk), bf16),
            pltpu.VMEM((rows, width), bf16),
            dma((2, 2, RING * RING, 2)),
            dma((2, 2, RING * RING, 2)),
            dma((2, 2)),
            dma((2, 2)),
            dma((2, 2)),
            dma((2,)),
            dma((2, PARTS)),
            dma((PARTS,)),
            dma((PARTS,)),
            dma((PARTS,)),
            dma((2, PARTS)),
            dma((PARTS,)),
            pltpu.SemaphoreType.REGULAR,
        ],
        compiler_params=pltpu.CompilerParams(
            collective_id=0, has_side_effects=True, vmem_limit_bytes=60 * 1024 * 1024
        ),
        name="layers",
    )(
        tokens[0].reshape(rows, width),
        docs.reshape(seq, 1),
        docs.reshape(1, seq),
        pos.reshape(seq, 1),
        pos.reshape(1, seq),
        norm_gain,
        w_query[0],
        w_out[0].T,
        w_key[0],
        w_value[0],
    )
    return state.reshape(1, 1, n_segments, quarter, width)


def solution(mesh):
    in_specs = (
        P("dp", None, "tensor", None),
        P("dp", None),
        P("section", None),
        P("section", "dp", "tensor"),
        P("section", None, "tensor"),
        P("section", None, "tensor"),
        P("section", "tensor", "dp"),
    )
    out_specs = P("section", "dp", None, "tensor", None)
    return jax.shard_map(
        on_device, mesh=mesh, in_specs=in_specs, out_specs=out_specs, check_vma=False
    )
```

```python
import jax
import jax.numpy as jnp
from jax import lax
from jax.experimental import pallas as pl
from jax.experimental.pallas import tpu as pltpu
from jax.sharding import PartitionSpec as P

HEAD = 128
MESH = pl.DeviceIdType.MESH
RING = 4
PARTS = 8
ORDER = (0, 1, 3, 2)

START, SPREAD, CROSS, RELAY, LAST = range(5)
CROSS_LAST = (((0, 3), (0, 3)), ((3, 1), (0,)))
Q_EVENTS = (
    (1, 0, 3), (1, 0, 1), (2, 0, 0), (1, 1, 3), (1, 1, 1), (3, 1, 0, 0, 3), (3, 1, 0, 0, 1), (2, 1, 0),
    (3, 0, 0, 0, 3), (3, 0, 0, 0, 1), (1, 0, 2), (2, 0, 3), (3, 0, 3, 0, 3), (3, 0, 3, 0, 1), (3, 1, 3, 0, 1),
    (3, 1, 3, 0, 3), (2, 0, 1), (3, 0, 1, 0, 3), (3, 0, 1, 0, 1), (3, 1, 1, 0, 1), (3, 1, 1, 0, 3), (2, 1, 3),
    (4, 1, 0), (1, 1, 2), (2, 1, 1), (4, 0, 0), (4, 1, 3), (3, 0, 2, 0, 1), (2, 0, 2), (3, 0, 2, 0, 3),
    (3, 1, 2, 0, 1), (4, 0, 3), (2, 1, 2), (3, 0, 1, 1, 1), (3, 1, 2, 0, 3), (3, 1, 1, 1, 1), (3, 0, 1, 1, 3),
    (3, 1, 1, 1, 3), (3, 1, 2, 1, 1), (3, 0, 2, 1, 1), (3, 1, 2, 1, 3), (3, 0, 2, 1, 3),
)
O_EVENTS = (
    (2, 0, 0), (1, 0, 1), (1, 1, 1), (1, 0, 3), (1, 1, 3), (2, 1, 0), (3, 1, 0, 0, 1), (3, 0, 0, 0, 1),
    (3, 1, 0, 0, 3), (3, 0, 0, 0, 3), (2, 0, 1), (3, 0, 0, 1, 1), (3, 1, 1, 0, 1), (3, 1, 1, 0, 3), (3, 0, 0, 1, 3),
    (2, 1, 1), (1, 0, 2), (3, 0, 1, 0, 1), (3, 1, 3, 0, 1), (3, 0, 1, 0, 3), (2, 0, 3), (3, 1, 3, 0, 3),
    (3, 0, 3, 0, 1), (3, 0, 3, 0, 3), (2, 1, 3), (1, 1, 2), (4, 1, 0), (2, 0, 2), (3, 1, 1, 1, 1), (2, 1, 2),
    (3, 1, 1, 1, 3), (3, 0, 2, 0, 1), (3, 1, 3, 1, 1), (3, 0, 2, 0, 3), (3, 1, 2, 0, 1), (4, 0, 1), (3, 1, 3, 1, 3),
    (3, 1, 2, 0, 3), (3, 1, 2, 1, 1), (3, 0, 2, 1, 1), (4, 0, 3), (3, 1, 2, 1, 3), (3, 0, 2, 1, 3),
)


def needs_and_sends(w, event):
    if event[0] == START:
        sends = []
        for cls in (0, 1):
            own = (w, cls, 0, 0, 0, None)
            sends += [(own, 0, 1), (own, 0, -1), (own, 2, 0)]
        for cls in (0, 1):
            own = (w, cls, 0, 0, 0, None)
            sends += [(own, 1, 1), (own, 1, -1)]
        return [], sends
    cls, fo = event[1:3]
    if event[0] == SPREAD:
        whole = (w, cls, 0, fo, 0, None)
        needs = [whole] if fo != 2 else [whole[:5] + (0,), whole[:5] + (1,)]
        sends = []
        if fo == 3:
            sends.append((whole[:5] + (0,), 0, 1))
        if fo == 1:
            sends.append((whole[:5] + (1,), 0, -1))
        return needs, sends + [(whole, 2, 0), (whole, 1, 1), (whole, 1, -1)]
    if event[0] == CROSS:
        whole = (w, cls, 1, fo, 0, None)
        return [whole], [(whole, 1, 1), (whole, 1, -1)]
    if event[0] == RELAY:
        who, go = event[3:]
        whole = (w, cls, who, fo, go, None)
        return [whole], [(whole[:5] + (0 if go == 3 else 1,), 1, 1 if go == 3 else -1)]
    whole = (w, cls, 0, fo, 2, None)
    return [whole[:5] + (0,), whole[:5] + (1,)], [(whole, 2, 0)]


def landing(piece, link, step):
    w, cls, who, fo, go, h = piece
    if link == 0:
        return (w, cls, who, (fo - step) % RING, go, h)
    if link == 1:
        return (w, cls, who, fo, (go - step) % RING, h)
    return (w, cls, 1 - who, fo, go, h)


def in_slab(piece, offset):
    return (piece[3] if piece[1] == 0 else piece[4]) == offset


def layer_kernel(
    tok, docs_col, docs_row, pos_col, pos_row, gain, wq, wot, wk, wv, out,
    full_q, full_o, kv_w, hidden, scaled, level, acc_q, acc_kv, query, kv_made, kv, attended, bias, part, part_in, fresh,
    w_recv, w_send, own_sem, swap_send, kvw_sem, kv_sem, kv_send, h_sem, h_send, p_recv, p_send, n_send, o_sem, gate,
):
    section = lax.axis_index("section")
    dp = lax.axis_index("dp")
    tensor = lax.axis_index("tensor")
    z, y, far = dp // 8, (dp // 2) % RING, dp % 2
    rows, width = tok.shape
    seq = 2 * rows
    block, q_width = wq.shape
    half = block // 2
    small = half // 32 * 16
    chunk = width // PARTS
    slab = 2 * chunk
    kv_width = wk.shape[1]
    weights = (full_q, full_o)
    shards = (wq, wot)

    def at(dz, dy):
        return (section, ((z + dz) % RING) * 8 + ((y + dy) % RING) * 2 + far, tensor)

    opposite = (section, z * 8 + y * 2 + (1 - far), 1 - tensor)
    partner = (section, dp, 1 - tensor)
    core = (1 - section, dp, tensor)
    partner_core = (1 - section, dp, 1 - tensor)
    peers = [at(1, 0), at(-1, 0), at(0, 1), at(0, -1), opposite, partner, core, partner_core]
    barrier = pltpu.get_barrier_semaphore()
    for peer in peers:
        pl.semaphore_signal(barrier, inc=1, device_id=peer, device_id_type=MESH)

    def place(piece):
        w, cls, who, fo, go, h = piece
        dz, dy = (fo, go) if cls == 0 else (go, fo)
        whose = far if who == 0 else 1 - far
        first = (((z + dz) % RING) * 8 + ((y + dy) % RING) * 2 + whose) * block + cls * half
        large = half - small
        cut = large if who == 0 else small
        size = half
        if h == 0:
            size = cut
        if h == 1:
            first, size = first + cut, half - cut
        return weights[w].at[pl.ds(pl.multiple_of(first, 16), size), :]

    def number(piece):
        w, cls, who, fo, go, h = piece
        return w, cls, who, fo * RING + go, 1 if h == 1 else 0

    def copy_of(piece, link, step):
        name = landing(piece, link, step)
        if link == 2:
            target = opposite
        else:
            target = at(step, 0) if link == piece[1] else at(0, step)
        return pltpu.make_async_remote_copy(
            src_ref=place(piece), dst_ref=place(piece), send_sem=w_send.at[number(name)],
            recv_sem=w_recv.at[number(name)], device_id=target, device_id_type=MESH,
        )

    def await_piece(piece):
        ref = place(piece)
        pltpu.make_async_copy(ref, ref, w_recv.at[number(piece)]).wait()

    def own_copy(w, cls):
        return pltpu.make_async_copy(
            shards[w].at[pl.ds(cls * half, half), :], place((w, cls, 0, 0, 0, None)), own_sem.at[w, cls]
        )

    def swap_copy(w, cls):
        return pltpu.make_async_remote_copy(
            src_ref=shards[w].at[pl.ds(cls * half, half), :], dst_ref=place((w, cls, 0, 0, 0, None)),
            send_sem=swap_send.at[w, cls], recv_sem=own_sem.at[w, cls], device_id=partner, device_id_type=MESH,
        )

    def signal_core():
        @pl.when(section == 0)
        def _():
            pl.semaphore_signal(gate, inc=1, device_id=core, device_id_type=MESH)

    def run(w, event):
        needs, sends = needs_and_sends(w, event)
        if event[0] == START:
            for cls in (0, 1):
                own_copy(w, cls).wait()
        for piece in needs:
            await_piece(piece)
        for send in sends:
            copy_of(*send).start()

    events = ([(START,)] + list(Q_EVENTS), [(START,)] + list(O_EVENTS))
    all_sends = [send for w in (0, 1) for event in events[w] for send in needs_and_sends(w, event)[1]]
    awaited = {piece for w in (0, 1) for event in events[w] for piece in needs_and_sends(w, event)[0]}

    def rest_of(w, offset):
        for send in all_sends:
            name = landing(*send)
            if name[0] == w and name not in awaited and in_slab(name, offset):
                await_piece(name)

    def rows_of(which):
        return pl.ds(pl.multiple_of(which * rows, 16), rows)

    def cols_of(k):
        first = ((z + ORDER[k // 2]) % RING) * slab + (k % 2) * chunk
        return pl.ds(pl.multiple_of(first, 128), chunk)

    def slab_of(j):
        return pl.ds(pl.multiple_of(((z + ORDER[j]) % RING) * slab, 128), slab)

    kvw_copies = [
        pltpu.make_async_copy(wk, kv_w.at[0], kvw_sem.at[0]),
        pltpu.make_async_copy(wv, kv_w.at[1], kvw_sem.at[1]),
    ]

    def token_copy(k):
        return pltpu.make_async_copy(
            tok.at[:, cols_of(k)], hidden.at[rows_of(tensor), cols_of(k)], h_sem.at[0, k]
        )

    def token_send(k):
        return pltpu.make_async_remote_copy(
            src_ref=tok.at[:, cols_of(k)], dst_ref=hidden.at[rows_of(tensor), cols_of(k)],
            send_sem=h_send.at[k], recv_sem=h_sem.at[1, k], device_id=partner, device_id_type=MESH,
        )

    def swap(w):
        @pl.when(far == 1)
        def _():
            for cls in (0, 1):
                swap_copy(w, cls).start()

    @pl.when(far == 0)
    def _():
        for w in (0, 1):
            for cls in (0, 1):
                own_copy(w, cls).start()

    pl.semaphore_wait(barrier, len(peers))

    @pl.when(section == 0)
    def _():
        swap(0)
        for k in range(PARTS):
            if k == PARTS - 2:
                swap(1)
            token_copy(k).start()
            token_send(k).start()

    for copy in kvw_copies:
        copy.start()

    allowed = (pos_row[...] <= pos_col[...]) & (docs_row[...] == docs_col[...])
    bias[...] = jnp.where(allowed, 0.0, -1e30)
    for copy in kvw_copies:
        copy.wait()

    step_rows = 32

    def prepare(j):
        for k in (2 * j, 2 * j + 1):
            for src, whose in ((0, tensor), (1, 1 - tensor)):
                ref = hidden.at[rows_of(whose), cols_of(k)]
                pltpu.make_async_copy(ref, ref, h_sem.at[src, k]).wait()
        cols = slab_of(j)

        def body(i, carry):
            here = pl.ds(pl.multiple_of(i * step_rows, step_rows), step_rows)
            wide = hidden[here, cols].astype(jnp.float32)
            scaled[j, here, :] = (wide * gain[:, cols]).astype(jnp.bfloat16)
            total = jnp.sum(wide * wide, axis=-1, keepdims=True)
            level[here, :] = total if j == 0 else level[here, :] + total
            return carry

        lax.fori_loop(0, seq // step_rows, body, 0)
        for i in (0, 1):
            cols_i = pl.ds(i * kv_width, kv_width)
            term = jnp.dot(scaled[j], kv_w[i, slab_of(j), :], preferred_element_type=jnp.float32)
            acc_kv[:, cols_i] = term if j == 0 else acc_kv[:, cols_i] + term

    tile = 256

    def project(j):
        def body(i, carry):
            cols = pl.ds(pl.multiple_of(i * tile, tile), tile)
            term = jnp.dot(scaled[j], full_q[slab_of(j), cols], preferred_element_type=jnp.float32)
            acc_q[:, cols] = term if j == 0 else acc_q[:, cols] + term
            return carry

        lax.fori_loop(0, q_width // tile, body, 0)

    def kv_exchange(i):
        return pltpu.make_async_remote_copy(
            src_ref=kv_made.at[i], dst_ref=kv.at[i], send_sem=kv_send.at[i], recv_sem=kv_sem.at[i],
            device_id=partner, device_id_type=MESH,
        )

    def kv_keep(i):
        return pltpu.make_async_copy(kv_made.at[i], kv.at[i], kv_sem.at[i])

    def finish_kv():
        factor = lax.rsqrt(level[...] / width + 1e-06)
        level[...] = factor
        for i in (0, 1):
            kv_made[i] = (acc_kv[:, i * kv_width : (i + 1) * kv_width] * factor).astype(jnp.bfloat16)

            @pl.when(far == 1)
            def _():
                kv_exchange(i).start()

            @pl.when(far == 0)
            def _():
                kv_keep(i).start()

    def finish_q():
        for i in range(q_width // tile):
            query[:, i * tile : (i + 1) * tile] = (acc_q[:, i * tile : (i + 1) * tile] * level[...]).astype(jnp.bfloat16)

    early = 24

    @pl.when(section == 0)
    def _():
        q_events, o_events = list(events[0]), list(events[1])

        def pump(w, count):
            todo = (q_events, o_events)[w]
            for _ in range(min(count, len(todo))):
                run(w, todo.pop(0))

        pump(0, 1 + 20)
        prepare(0)
        pump(0, 8)
        prepare(1)
        pump(0, 6)
        prepare(2)
        pump(0, len(q_events))
        pump(1, 1)
        prepare(3)
        signal_core()
        finish_kv()
        for j in range(RING):
            rest_of(0, ORDER[j])
            project(j)
            pump(1, 4)
        finish_q()
        pump(1, early - 17)

    @pl.when(section == 1)
    def _():
        pl.semaphore_wait(gate, 1)
        for w in (0, 1):
            swap(w)
        pl.semaphore_wait(gate, 1)
        q_events, o_events = list(events[0]), list(events[1])

        def pump(w, count):
            todo = (q_events, o_events)[w]
            for _ in range(min(count, len(todo))):
                run(w, todo.pop(0))

        pump(0, 1 + 30)
        prepare(0)
        pump(0, len(q_events))
        pump(1, 1)
        prepare(1)
        pump(1, 3)
        for j in range(RING):
            if j >= 2:
                prepare(j)
            if j == 3:
                finish_kv()
            rest_of(0, ORDER[j])
            project(j)
            pump(1, 4)
        finish_q()
        pump(1, early - 20)

    todo = list(events[1])[early:]

    def pump(count):
        for _ in range(min(count, len(todo))):
            run(1, todo.pop(0))

    scale = 1.0 / HEAD**0.5
    heads = q_width // HEAD
    group = heads // (kv_width // HEAD)

    def attend(n, h):
        cols = pl.ds(pl.multiple_of(h * HEAD, HEAD), HEAD)
        kv_cols = pl.ds(n * HEAD, HEAD)
        scores = lax.dot_general(
            query[:, cols], kv[0, :, kv_cols], (((1,), (1,)), ((), ())), preferred_element_type=jnp.float32
        )
        scores = scores * scale + bias[...]
        scores = jnp.exp(scores - jnp.max(scores, axis=-1, keepdims=True))
        mix = (scores / jnp.sum(scores, axis=-1, keepdims=True)).astype(jnp.bfloat16)
        attended[:, cols] = jnp.dot(
            mix, kv[1, :, kv_cols], preferred_element_type=jnp.float32
        ).astype(jnp.bfloat16)

    for i in (0, 1):
        kv_keep(i).wait()
    for n in range(heads // group):
        for lo, hi in ((0, 3), (3, group)):
            lax.fori_loop(n * group + lo, n * group + hi, lambda h, c, n=n: (attend(n, h), c)[1], 0)
            pump(2)

    def part_send(k):
        return pltpu.make_async_remote_copy(
            src_ref=part.at[k, rows_of(1 - tensor), :], dst_ref=part_in.at[k],
            send_sem=p_send.at[k], recv_sem=p_recv.at[k], device_id=partner, device_id_type=MESH,
        )

    def out_copy(k):
        return pltpu.make_async_copy(fresh.at[:, cols_of(k)], out.at[:, cols_of(k)], o_sem.at[k])

    def next_send(k, side):
        return pltpu.make_async_remote_copy(
            src_ref=fresh.at[:, cols_of(k)], dst_ref=hidden.at[rows_of(tensor), cols_of(k)],
            send_sem=n_send.at[side, k], recv_sem=h_sem.at[side, k],
            device_id=core if side == 0 else partner_core, device_id_type=MESH,
        )

    def finish(k):
        part_send(k).wait_recv()
        own = hidden[rows_of(tensor), cols_of(k)].astype(jnp.float32)
        update = part[k, rows_of(tensor), :].astype(jnp.float32) + part_in[k].astype(jnp.float32)
        fresh[:, cols_of(k)] = (own + update).astype(jnp.bfloat16)
        out_copy(k).start()

        @pl.when(section == 0)
        def _():
            next_send(k, 0).start()
            next_send(k, 1).start()

    def waits_in(event, offset):
        return any(in_slab(piece, offset) for piece in needs_and_sends(1, event)[0])

    for k in range(PARTS):
        if k % 2 == 0:
            while any(waits_in(event, ORDER[k // 2]) for event in todo):
                pump(1)
            if k == 2:
                pump(len(todo))
                signal_core()
            rest_of(1, ORDER[k // 2])
        result = lax.dot_general(
            attended[...], full_o[cols_of(k), :], (((1,), (1,)), ((), ())), preferred_element_type=jnp.float32
        )
        part[k] = result.astype(jnp.bfloat16)
        part_send(k).start()
        if k >= 2:
            finish(k - 2)
    finish(PARTS - 2)
    finish(PARTS - 1)

    for send in all_sends:
        copy_of(*send).wait_send()
    for k in range(PARTS):
        part_send(k).wait_send()
        out_copy(k).wait()

    @pl.when(far == 1)
    def _():
        for w in (0, 1):
            for cls in (0, 1):
                swap_copy(w, cls).wait_send()
        for i in (0, 1):
            kv_exchange(i).wait_send()

    @pl.when(section == 0)
    def _():
        for k in range(PARTS):
            token_send(k).wait_send()
            next_send(k, 0).wait_send()
            next_send(k, 1).wait_send()


def on_device(tokens, doc_ids, norm_gain, w_query, w_key, w_value, w_out):
    n_segments, quarter, width = tokens.shape[1:]
    rows = n_segments * quarter
    seq = 2 * rows
    block, q_width = w_query.shape[1:]
    kv_width = w_key.shape[2]
    chunk = width // PARTS
    docs = doc_ids[0].reshape(n_segments, 2, quarter).transpose(1, 0, 2).reshape(seq)
    pos = jnp.arange(seq, dtype=jnp.int32).reshape(n_segments, 2, quarter).transpose(1, 0, 2).reshape(seq)
    bf16, f32 = jnp.bfloat16, jnp.float32
    dma = pltpu.SemaphoreType.DMA
    anywhere = pl.BlockSpec(memory_space=pl.ANY)
    vmem = pl.BlockSpec(memory_space=pltpu.VMEM)
    state = pl.pallas_call(
        layer_kernel,
        out_shape=jax.ShapeDtypeStruct((rows, width), bf16),
        in_specs=[anywhere] + [vmem] * 5 + [anywhere] * 4,
        out_specs=anywhere,
        scratch_shapes=[
            pltpu.VMEM((width, q_width), bf16),
            pltpu.VMEM((width, q_width), bf16),
            pltpu.VMEM((2, width, kv_width), bf16),
            pltpu.VMEM((seq, width), bf16),
            pltpu.VMEM((RING, seq, 2 * chunk), bf16),
            pltpu.VMEM((seq, 1), f32),
            pltpu.VMEM((seq, q_width), f32),
            pltpu.VMEM((seq, 2 * kv_width), f32),
            pltpu.VMEM((seq, q_width), bf16),
            pltpu.VMEM((2, seq, kv_width), bf16),
            pltpu.VMEM((2, seq, kv_width), bf16),
            pltpu.VMEM((seq, q_width), bf16),
            pltpu.VMEM((seq, seq), f32),
            pltpu.VMEM((PARTS, seq, chunk), bf16),
            pltpu.VMEM((PARTS, rows, chunk), bf16),
            pltpu.VMEM((rows, width), bf16),
            dma((2, 2, 2, RING * RING, 2)),
            dma((2, 2, 2, RING * RING, 2)),
            dma((2, 2)),
            dma((2, 2)),
            dma((2,)),
            dma((2,)),
            dma((2,)),
            dma((2, PARTS)),
            dma((PARTS,)),
            dma((PARTS,)),
            dma((PARTS,)),
            dma((2, PARTS)),
            dma((PARTS,)),
            pltpu.SemaphoreType.REGULAR,
        ],
        compiler_params=pltpu.CompilerParams(
            collective_id=0, has_side_effects=True, vmem_limit_bytes=60 * 1024 * 1024
        ),
        name="layers",
    )(
        tokens[0].reshape(rows, width),
        docs.reshape(seq, 1),
        docs.reshape(1, seq),
        pos.reshape(seq, 1),
        pos.reshape(1, seq),
        norm_gain,
        w_query[0],
        w_out[0].T,
        w_key[0],
        w_value[0],
    )
    return state.reshape(1, 1, n_segments, quarter, width)


def solution(mesh):
    in_specs = (
        P("dp", None, "tensor", None),
        P("dp", None),
        P("section", None),
        P("section", "dp", "tensor"),
        P("section", None, "tensor"),
        P("section", None, "tensor"),
        P("section", "tensor", "dp"),
    )
    out_specs = P("section", "dp", None, "tensor", None)
    return jax.shard_map(
        on_device, mesh=mesh, in_specs=in_specs, out_specs=out_specs, check_vma=False
    )
```

```python
import functools

import jax
import jax.numpy as jnp
from jax import lax
from jax.experimental import pallas as pl
from jax.experimental.pallas import tpu as pltpu
from jax.sharding import PartitionSpec as P

HEAD = 128
MESH = pl.DeviceIdType.MESH
RING = 4
PARTS = 8
ORDER = (0, 1, 3, 2)

START, SPREAD, CROSS, RELAY, LAST, UNIT = range(6)
SIGNAL, AWAIT = 12, 13
PROGRAMS = (
    (
        (0, 0, 0), (0, 0, 1), (1, 0, 0, 3), (1, 0, 1, 1), (1, 0, 1, 3), (1, 0, 0, 1), (2, 0, 1, 0),
        (3, 0, 0, 0, 0, 1), (3, 0, 0, 3, 0, 1), (2, 0, 0, 0), (1, 0, 1, 2), (5, 0), (3, 0, 1, 3, 0, 1),
        (3, 0, 0, 0, 0, 3), (3, 0, 1, 1, 0, 1), (3, 0, 1, 3, 0, 3), (1, 0, 0, 2), (2, 0, 0, 1), (3, 0, 0, 3, 0, 3),
        (3, 0, 0, 1, 0, 3), (2, 0, 1, 1), (5, 1), (3, 0, 0, 2, 0, 1), (2, 0, 0, 3), (3, 0, 1, 0, 0, 3),
        (3, 0, 1, 2, 0, 3), (2, 0, 1, 2), (3, 0, 1, 2, 0, 1), (4, 0, 0, 0), (4, 0, 1, 3), (2, 0, 1, 3),
        (3, 0, 0, 1, 0, 1), (2, 0, 0, 2), (3, 0, 1, 0, 0, 1), (4, 0, 0, 3), (3, 0, 1, 1, 1, 3), (3, 0, 0, 1, 1, 3),
        (5, 2), (12, 0), (3, 0, 0, 1, 1, 1), (5, 3), (0, 1, 0), (4, 0, 1, 0), (0, 1, 1), (3, 0, 1, 1, 0, 3),
        (6, 0, 0), (3, 0, 1, 2, 1, 1), (3, 0, 0, 2, 0, 3), (3, 1, 0, 0, 0, 1), (3, 0, 1, 2, 1, 3), (7,),
        (3, 0, 1, 1, 1, 1), (3, 0, 0, 2, 1, 3), (1, 1, 0, 1), (6, 2, 0), (1, 1, 1, 3), (1, 1, 1, 1),
        (3, 0, 0, 2, 1, 1), (6, 0, 1), (6, 1, 0), (1, 1, 0, 3), (2, 1, 1, 0), (6, 2, 1), (3, 1, 1, 0, 0, 3),
        (2, 1, 0, 0), (6, 1, 1), (3, 1, 0, 1, 0, 1), (6, 3, 0), (3, 1, 1, 3, 0, 3), (1, 1, 1, 2), (6, 3, 1),
        (3, 1, 0, 0, 0, 3), (3, 1, 0, 3, 0, 1), (2, 1, 1, 3), (3, 1, 0, 3, 0, 3), (8,), (3, 1, 0, 1, 0, 3),
        (2, 1, 1, 1), (9, 0), (9, 1), (3, 1, 0, 0, 1, 1), (3, 1, 0, 0, 1, 3), (1, 1, 0, 2), (2, 1, 0, 1), (9, 2),
        (9, 3), (9, 4), (2, 1, 1, 2), (10, 0), (4, 1, 0, 1), (2, 1, 0, 2), (3, 1, 1, 2, 0, 3), (3, 1, 1, 1, 0, 1),
        (3, 1, 1, 3, 0, 1), (10, 1), (3, 1, 1, 2, 0, 1), (3, 1, 0, 2, 0, 1), (12, 1), (4, 1, 0, 3), (4, 1, 1, 3),
        (3, 1, 0, 2, 1, 1), (3, 1, 1, 1, 1, 3), (3, 1, 1, 1, 0, 3), (3, 1, 0, 2, 0, 3), (11, 0), (3, 1, 1, 0, 0, 1),
        (3, 1, 1, 1, 1, 1), (3, 1, 0, 2, 1, 3), (2, 1, 0, 3), (3, 1, 1, 2, 1, 3), (3, 1, 1, 2, 1, 1), (11, 1),
        (10, 2), (10, 3), (4, 1, 1, 0), (10, 4), (10, 5), (10, 6), (10, 7), (11, 3), (11, 2), (11, 4), (11, 5),
        (11, 6), (11, 7),
    ),
    (
        (0, 0, 1), (0, 0, 0), (1, 0, 0, 3), (1, 0, 1, 1), (1, 0, 0, 1), (3, 0, 0, 0, 0, 1), (1, 0, 1, 3),
        (3, 0, 1, 0, 0, 3), (0, 1, 1), (1, 0, 0, 2), (5, 0), (3, 0, 1, 3, 0, 1), (3, 0, 0, 0, 0, 3), (2, 0, 1, 1),
        (2, 0, 0, 1), (3, 0, 0, 3, 0, 3), (0, 1, 0), (3, 0, 0, 2, 0, 1), (1, 0, 1, 2), (4, 0, 0, 0),
        (3, 0, 0, 3, 0, 1), (2, 0, 0, 0), (3, 0, 1, 0, 0, 1), (2, 0, 0, 2), (2, 0, 1, 0), (3, 0, 1, 3, 0, 3),
        (3, 1, 0, 0, 0, 1), (1, 1, 0, 1), (4, 0, 0, 3), (2, 1, 0, 0), (2, 0, 0, 3), (3, 0, 1, 1, 1, 1),
        (3, 0, 1, 1, 0, 1), (1, 1, 1, 3), (2, 0, 1, 2), (2, 0, 1, 3), (3, 0, 1, 2, 0, 1), (3, 0, 1, 1, 0, 3), (5, 1),
        (3, 0, 0, 1, 0, 3), (3, 0, 0, 2, 0, 3), (3, 0, 0, 1, 0, 1), (6, 0, 0), (3, 0, 0, 1, 1, 3),
        (3, 0, 0, 1, 1, 1), (3, 0, 0, 2, 1, 1), (4, 0, 1, 3), (6, 0, 1), (3, 0, 0, 2, 1, 3), (4, 0, 1, 0),
        (1, 1, 0, 3), (3, 1, 0, 0, 1, 3), (3, 1, 1, 3, 0, 1), (3, 0, 1, 2, 0, 3), (3, 0, 1, 2, 1, 3), (1, 1, 1, 1),
        (3, 0, 1, 1, 1, 3), (5, 2), (3, 1, 1, 0, 0, 1), (3, 1, 1, 3, 0, 3), (6, 2, 0), (3, 0, 1, 2, 1, 1),
        (3, 1, 0, 1, 0, 1), (2, 1, 1, 3), (3, 1, 0, 0, 0, 3), (3, 1, 0, 0, 1, 1), (5, 3), (7,), (3, 1, 1, 0, 0, 3),
        (2, 1, 0, 1), (6, 2, 1), (6, 1, 0), (2, 1, 1, 0), (3, 1, 0, 1, 0, 3), (6, 3, 0), (6, 1, 1), (1, 1, 1, 2),
        (6, 3, 1), (8,), (2, 1, 1, 1), (1, 1, 0, 2), (9, 0), (9, 1), (2, 1, 1, 2), (9, 2), (9, 3), (9, 4), (10, 0),
        (3, 1, 1, 1, 0, 1), (3, 1, 0, 3, 0, 3), (3, 1, 1, 1, 1, 3), (3, 1, 1, 1, 1, 1), (3, 1, 0, 2, 0, 1),
        (3, 1, 1, 1, 0, 3), (3, 1, 0, 3, 0, 1), (3, 1, 1, 2, 0, 1), (4, 1, 0, 1), (2, 1, 0, 3), (3, 1, 0, 2, 0, 3),
        (2, 1, 0, 2), (3, 1, 1, 2, 0, 3), (3, 1, 1, 2, 1, 1), (10, 1), (4, 1, 0, 3), (4, 1, 1, 3), (4, 1, 1, 0),
        (10, 2), (3, 1, 1, 2, 1, 3), (10, 3), (11, 1), (3, 1, 0, 2, 1, 3), (10, 4), (11, 0), (10, 5),
        (3, 1, 0, 2, 1, 1), (11, 2), (10, 6), (10, 7), (11, 4), (11, 5), (11, 6), (11, 3), (11, 7),
    ),
)


def needs_and_sends(event):
    kind, w, cls = event[:3]
    if kind == START:
        own = (w, cls, 0, 0, 0, None)
        return [], [(own, 0, 1), (own, 0, -1), (own, 2, 0), (own, 1, 1), (own, 1, -1)]
    fo = event[3]
    if kind == SPREAD:
        whole = (w, cls, 0, fo, 0, None)
        needs = [whole] if fo != 2 else [whole[:5] + (0,), whole[:5] + (1,)]
        sends = []
        if fo == 3:
            sends.append((whole[:5] + (0,), 0, 1))
        if fo == 1:
            sends.append((whole[:5] + (1,), 0, -1))
        return needs, sends + [(whole, 2, 0), (whole, 1, 1), (whole, 1, -1)]
    if kind == CROSS:
        whole = (w, cls, 1, fo, 0, None)
        return [whole], [(whole, 1, 1), (whole, 1, -1)]
    if kind == RELAY:
        who, go = event[4:]
        whole = (w, cls, who, fo, go, None)
        return [whole], [(whole[:5] + (0 if go == 3 else 1,), 1, 1 if go == 3 else -1)]
    whole = (w, cls, 0, fo, 2, None)
    return [whole[:5] + (0,), whole[:5] + (1,)], [(whole, 2, 0)]


def landing(piece, link, step):
    w, cls, who, fo, go, h = piece
    if link == 0:
        return (w, cls, who, (fo - step) % RING, go, h)
    if link == 1:
        return (w, cls, who, fo, (go - step) % RING, h)
    return (w, cls, 1 - who, fo, go, h)


def in_slab(piece, offset):
    return (piece[3] if piece[1] == 0 else piece[4]) == offset


def layer_kernel(
    quarter, tok, docs, gain, wq, wot, wk, wv, out,
    full_q, full_o, kv_w, hidden, scaled, level, acc_q, acc_kv, query, kv_made, kv, attended, bias, part, part_in,
    w_recv, w_send, own_sem, swap_send, kvw_sem, kv_sem, kv_send, h_sem, h_send, p_recv, p_send, n_send, gate,
):
    section = lax.axis_index("section")
    dp = lax.axis_index("dp")
    tensor = lax.axis_index("tensor")
    z, y, far = dp // 8, (dp // 2) % RING, dp % 2
    rows, width = tok.shape
    seq = 2 * rows
    block, q_width = wq.shape
    half = block // 2
    small = half // 32 * 16
    chunk = width // PARTS
    slab = 2 * chunk
    kv_width = wk.shape[1]
    weights = (full_q, full_o)
    shards = (wq, wot)

    z_of = [lax.rem(z + d, RING) * 8 for d in range(RING)]
    y_of = [lax.rem(y + d, RING) * 2 for d in range(RING)]
    whose_of = [far, 1 - far]
    z_row, y_row, x_row = ([dp_part * block for dp_part in parts] for parts in (z_of, y_of, whose_of))

    def at(dz, dy):
        return (section, z_of[dz % RING] + y_of[dy % RING] + far, tensor)

    opposite = (section, z_of[0] + y_of[0] + (1 - far), 1 - tensor)
    partner = (section, dp, 1 - tensor)
    core = (1 - section, dp, tensor)
    partner_core = (1 - section, dp, 1 - tensor)
    peers = [at(1, 0), at(-1, 0), at(0, 1), at(0, -1), opposite, partner, core, partner_core]
    barrier = pltpu.get_barrier_semaphore()
    for peer in peers:
        pl.semaphore_signal(barrier, inc=1, device_id=peer, device_id_type=MESH)

    def place(piece):
        w, cls, who, fo, go, h = piece
        dz, dy = (fo, go) if cls == 0 else (go, fo)
        first = z_row[dz] + y_row[dy] + x_row[who] + cls * half
        large = half - small
        cut = large if who == 0 else small
        size = half
        if h == 0:
            size = cut
        if h == 1:
            first, size = first + cut, half - cut
        return weights[w].at[pl.ds(pl.multiple_of(first, 16), size), :]

    def number(piece):
        w, cls, who, fo, go, h = piece
        return w, cls, who, fo * RING + go, 1 if h == 1 else 0

    def copy_of(piece, link, step):
        name = landing(piece, link, step)
        if link == 2:
            target = opposite
        else:
            target = at(step, 0) if link == piece[1] else at(0, step)
        return pltpu.make_async_remote_copy(
            src_ref=place(piece), dst_ref=place(piece), send_sem=w_send.at[number(name)],
            recv_sem=w_recv.at[number(name)], device_id=target, device_id_type=MESH,
        )

    def await_piece(piece):
        ref = place(piece)
        pltpu.make_async_copy(ref, ref, w_recv.at[number(piece)]).wait()

    def own_copy(w, cls):
        return pltpu.make_async_copy(
            shards[w].at[pl.ds(cls * half, half), :], place((w, cls, 0, 0, 0, None)), own_sem.at[w, cls]
        )

    def swap_copy(w, cls):
        return pltpu.make_async_remote_copy(
            src_ref=shards[w].at[pl.ds(cls * half, half), :], dst_ref=place((w, cls, 0, 0, 0, None)),
            send_sem=swap_send.at[w, cls], recv_sem=own_sem.at[w, cls], device_id=partner, device_id_type=MESH,
        )

    def signal_core():
        @pl.when(section == 0)
        def _():
            pl.semaphore_signal(gate, inc=1, device_id=core, device_id_type=MESH)

    def run(event):
        needs, sends = needs_and_sends(event)
        if event[0] == START:
            own_copy(*event[1:]).wait()
        for piece in needs:
            await_piece(piece)
        for send in sends:
            copy_of(*send).start()

    events = [step for step in PROGRAMS[0] if step[0] < UNIT]
    all_sends = [send for event in events for send in needs_and_sends(event)[1]]
    awaited = {piece for event in events for piece in needs_and_sends(event)[0]}

    def rest_of(w, offset):
        for send in all_sends:
            name = landing(*send)
            if name[0] == w and name not in awaited and in_slab(name, offset):
                await_piece(name)

    def rows_of(which):
        return pl.ds(pl.multiple_of(which * rows, 16), rows)

    def cols_of(k):
        first = ((z + ORDER[k // 2]) % RING) * slab + (k % 2) * chunk
        return pl.ds(pl.multiple_of(first, 128), chunk)

    def slab_of(j):
        return pl.ds(pl.multiple_of(((z + ORDER[j]) % RING) * slab, 128), slab)

    kvw_copies = [
        pltpu.make_async_copy(wk, kv_w.at[0], kvw_sem.at[0]),
        pltpu.make_async_copy(wv, kv_w.at[1], kvw_sem.at[1]),
    ]

    def token_copy(k):
        return pltpu.make_async_copy(
            tok.at[:, cols_of(k)], hidden.at[rows_of(tensor), cols_of(k)], h_sem.at[0, k]
        )

    def token_send(k):
        return pltpu.make_async_remote_copy(
            src_ref=tok.at[:, cols_of(k)], dst_ref=hidden.at[rows_of(tensor), cols_of(k)],
            send_sem=h_send.at[k], recv_sem=h_sem.at[1, k], device_id=partner, device_id_type=MESH,
        )

    def swap(w):
        @pl.when(far == 1)
        def _():
            for cls in (0, 1):
                swap_copy(w, cls).start()

    @pl.when(far == 0)
    def _():
        for w in (0, 1):
            for cls in (0, 1):
                own_copy(w, cls).start()

    pl.semaphore_wait(barrier, len(peers))

    @pl.when(section == 0)
    def _():
        swap(0)
        for k in range(PARTS):
            token_copy(k).start()
            token_send(k).start()
        swap(1)

    for copy in kvw_copies:
        copy.start()

    def settle():
        for copy in kvw_copies:
            copy.wait()

        def position(index):
            upper = jnp.where(index >= rows, 1, 0)
            segment = sum(jnp.where(index - rows * upper >= quarter * n, 1, 0) for n in range(1, rows // quarter))
            return index - upper * (rows - quarter) + segment * quarter

        here = position(lax.broadcasted_iota(jnp.int32, (seq, seq), 1))
        pick = jnp.where(lax.broadcasted_iota(jnp.int32, (seq, seq), 0) == here, 1.0, 0.0)
        along = jnp.broadcast_to(docs[...].astype(jnp.float32), (8, seq))
        docs_row = jnp.dot(along, pick, preferred_element_type=jnp.float32)[:1, :]
        there = position(lax.broadcasted_iota(jnp.int32, (seq, seq), 0))
        pick = lax.broadcasted_iota(jnp.int32, (seq, seq), 1) == there
        docs_col = jnp.sum(jnp.where(pick, docs[...].astype(jnp.float32), 0.0), axis=-1, keepdims=True)
        bias[...] = jnp.where((here <= there) & (docs_row == docs_col), 0.0, -1e30)

    step_rows = 32

    def prepare(j):
        for k in (2 * j, 2 * j + 1):
            for src, whose in ((0, tensor), (1, 1 - tensor)):
                ref = hidden.at[rows_of(whose), cols_of(k)]
                pltpu.make_async_copy(ref, ref, h_sem.at[src, k]).wait()
        cols = slab_of(j)

        def body(i, carry):
            here = pl.ds(pl.multiple_of(i * step_rows, step_rows), step_rows)
            wide = hidden[here, cols].astype(jnp.float32)
            scaled[j, here, :] = (wide * gain[:, cols]).astype(jnp.bfloat16)
            total = jnp.sum(wide * wide, axis=-1, keepdims=True)
            level[here, :] = total if j == 0 else level[here, :] + total
            return carry

        lax.fori_loop(0, seq // step_rows, body, 0)
        for i in (0, 1):
            cols_i = pl.ds(i * kv_width, kv_width)
            term = jnp.dot(scaled[j], kv_w[i, slab_of(j), :], preferred_element_type=jnp.float32)
            acc_kv[:, cols_i] = term if j == 0 else acc_kv[:, cols_i] + term

    tile = 256

    def project(j, part):
        if part == 0:
            rest_of(0, ORDER[j])

        def body(i, carry):
            cols = pl.ds(pl.multiple_of(i * tile, tile), tile)
            term = jnp.dot(scaled[j], full_q[slab_of(j), cols], preferred_element_type=jnp.float32)
            acc_q[:, cols] = term if j == 0 else acc_q[:, cols] + term
            return carry

        lax.fori_loop((0, 3)[part], (3, q_width // tile)[part], body, 0)

    def kv_exchange(i):
        return pltpu.make_async_remote_copy(
            src_ref=kv_made.at[i], dst_ref=kv.at[i], send_sem=kv_send.at[i], recv_sem=kv_sem.at[i],
            device_id=partner, device_id_type=MESH,
        )

    def kv_keep(i):
        return pltpu.make_async_copy(kv_made.at[i], kv.at[i], kv_sem.at[i])

    def finish_kv():
        factor = lax.rsqrt(level[...] / width + 1e-06)
        level[...] = factor
        for i in (0, 1):
            kv_made[i] = (acc_kv[:, i * kv_width : (i + 1) * kv_width] * factor).astype(jnp.bfloat16)

            @pl.when(far == 1)
            def _():
                kv_exchange(i).start()

            @pl.when(far == 0)
            def _():
                kv_keep(i).start()

    def finish_q():
        for i in range(q_width // tile):
            query[:, i * tile : (i + 1) * tile] = (acc_q[:, i * tile : (i + 1) * tile] * level[...]).astype(jnp.bfloat16)

    scale = 1.0 / HEAD**0.5
    heads = q_width // HEAD
    group = heads // (kv_width // HEAD)

    def attend(pair):
        if pair == 0:
            for i in (0, 1):
                kv_keep(i).wait()
        for h in (2 * pair, 2 * pair + 1):
            cols = slice(h * HEAD, (h + 1) * HEAD)
            kv_cols = slice(h // group * HEAD, (h // group + 1) * HEAD)
            scores = lax.dot_general(
                query[:, cols], kv[0, :, kv_cols], (((1,), (1,)), ((), ())), preferred_element_type=jnp.float32
            )
            scores = scores * scale + bias[...]
            scores = jnp.exp(scores - jnp.max(scores, axis=-1, keepdims=True))
            mix = (scores / jnp.sum(scores, axis=-1, keepdims=True)).astype(jnp.bfloat16)
            attended[:, cols] = jnp.dot(
                mix, kv[1, :, kv_cols], preferred_element_type=jnp.float32
            ).astype(jnp.bfloat16)

    def part_send(k):
        return pltpu.make_async_remote_copy(
            src_ref=part.at[k, rows_of(1 - tensor), :], dst_ref=part_in.at[k],
            send_sem=p_send.at[k], recv_sem=p_recv.at[k], device_id=partner, device_id_type=MESH,
        )

    def next_send(k, side):
        return pltpu.make_async_remote_copy(
            src_ref=out.at[:, cols_of(k)], dst_ref=hidden.at[rows_of(tensor), cols_of(k)],
            send_sem=n_send.at[side, k], recv_sem=h_sem.at[side, k],
            device_id=core if side == 0 else partner_core, device_id_type=MESH,
        )

    def finish(k):
        part_send(k).wait_recv()
        own = hidden[rows_of(tensor), cols_of(k)].astype(jnp.float32)
        update = part[k, rows_of(tensor), :].astype(jnp.float32) + part_in[k].astype(jnp.float32)
        out[:, cols_of(k)] = (own + update).astype(jnp.bfloat16)

        @pl.when(section == 0)
        def _():
            next_send(k, 0).start()
            next_send(k, 1).start()

    def multiply(k):
        if k % 2 == 0:
            rest_of(1, ORDER[k // 2])
        result = lax.dot_general(
            attended[...], full_o[cols_of(k), :], (((1,), (1,)), ((), ())), preferred_element_type=jnp.float32
        )
        part[k] = result.astype(jnp.bfloat16)
        part_send(k).start()

    units = (prepare, project, finish_kv, finish_q, attend, multiply, finish)

    def program(steps, settled):
        for step in steps:
            if step[0] < UNIT:
                run(step)
                continue
            if step[0] == SIGNAL:
                signal_core()
            elif step[0] == AWAIT:
                pl.semaphore_wait(gate, 1)
            else:
                if step == (UNIT, 0) and not settled:
                    settle()
                units[step[0] - UNIT](*step[1:])

    @pl.when(section == 0)
    def _():
        program(PROGRAMS[0], False)

    @pl.when(section == 1)
    def _():
        settle()
        pl.semaphore_wait(gate, 1)
        for w in (0, 1):
            swap(w)
        pl.semaphore_wait(gate, 1)
        program(PROGRAMS[1], True)

    for send in all_sends:
        copy_of(*send).wait_send()
    for k in range(PARTS):
        part_send(k).wait_send()

    @pl.when(far == 1)
    def _():
        for w in (0, 1):
            for cls in (0, 1):
                swap_copy(w, cls).wait_send()
        for i in (0, 1):
            kv_exchange(i).wait_send()

    @pl.when(section == 0)
    def _():
        for k in range(PARTS):
            token_send(k).wait_send()
            next_send(k, 0).wait_send()
            next_send(k, 1).wait_send()


def on_device(tokens, doc_ids, norm_gain, w_query, w_key, w_value, w_out):
    n_segments, quarter, width = tokens.shape[1:]
    rows = n_segments * quarter
    seq = 2 * rows
    block, q_width = w_query.shape[1:]
    kv_width = w_key.shape[2]
    chunk = width // PARTS
    bf16, f32 = jnp.bfloat16, jnp.float32
    dma = pltpu.SemaphoreType.DMA
    anywhere = pl.BlockSpec(memory_space=pl.ANY)
    vmem = pl.BlockSpec(memory_space=pltpu.VMEM)
    state = pl.pallas_call(
        functools.partial(layer_kernel, quarter),
        out_shape=pltpu.VMEM((rows, width), bf16),
        in_specs=[anywhere, vmem, vmem] + [anywhere] * 4,
        out_specs=vmem,
        scratch_shapes=[
            pltpu.VMEM((width, q_width), bf16),
            pltpu.VMEM((width, q_width), bf16),
            pltpu.VMEM((2, width, kv_width), bf16),
            pltpu.VMEM((seq, width), bf16),
            pltpu.VMEM((RING, seq, 2 * chunk), bf16),
            pltpu.VMEM((seq, 1), f32),
            pltpu.VMEM((seq, q_width), f32),
            pltpu.VMEM((seq, 2 * kv_width), f32),
            pltpu.VMEM((seq, q_width), bf16),
            pltpu.VMEM((2, seq, kv_width), bf16),
            pltpu.VMEM((2, seq, kv_width), bf16),
            pltpu.VMEM((seq, q_width), bf16),
            pltpu.VMEM((seq, seq), f32),
            pltpu.VMEM((PARTS, seq, chunk), bf16),
            pltpu.VMEM((PARTS, rows, chunk), bf16),
            dma((2, 2, 2, RING * RING, 2)),
            dma((2, 2, 2, RING * RING, 2)),
            dma((2, 2)),
            dma((2, 2)),
            dma((2,)),
            dma((2,)),
            dma((2,)),
            dma((2, PARTS)),
            dma((PARTS,)),
            dma((PARTS,)),
            dma((PARTS,)),
            dma((2, PARTS)),
            pltpu.SemaphoreType.REGULAR,
        ],
        compiler_params=pltpu.CompilerParams(
            collective_id=0, has_side_effects=True, vmem_limit_bytes=60 * 1024 * 1024
        ),
        name="layers",
    )(
        tokens[0].reshape(rows, width),
        doc_ids,
        norm_gain,
        w_query[0],
        w_out[0].T,
        w_key[0],
        w_value[0],
    )
    return state.reshape(1, 1, n_segments, quarter, width)


def solution(mesh):
    in_specs = (
        P("dp", None, "tensor", None),
        P("dp", None),
        P("section", None),
        P("section", "dp", "tensor"),
        P("section", None, "tensor"),
        P("section", None, "tensor"),
        P("section", "tensor", "dp"),
    )
    out_specs = P("section", "dp", None, "tensor", None)
    return jax.shard_map(
        on_device, mesh=mesh, in_specs=in_specs, out_specs=out_specs, check_vma=False
    )
```

```python
import functools

import jax
import jax.numpy as jnp
from jax import lax
from jax.experimental import pallas as pl
from jax.experimental.pallas import tpu as pltpu
from jax.sharding import PartitionSpec as P

HEAD = 128
MESH = pl.DeviceIdType.MESH
RING = 4
PARTS = 8
ORDER = (0, 1, 3, 2)

START, SPREAD, CROSS, RELAY, LAST, UNIT = range(6)
SIGNAL, AWAIT = 12, 13
PROGRAMS = (
    (
        (0, 0, 0), (0, 0, 1), (1, 0, 0, 3), (1, 0, 1, 1), (1, 0, 1, 3), (1, 0, 0, 1), (2, 0, 1, 0),
        (3, 0, 0, 0, 0, 1), (3, 0, 0, 3, 0, 1), (2, 0, 0, 0), (1, 0, 1, 2), (5, 0), (3, 0, 1, 3, 0, 1),
        (3, 0, 0, 0, 0, 3), (3, 0, 1, 1, 0, 1), (3, 0, 1, 3, 0, 3), (1, 0, 0, 2), (2, 0, 0, 1), (3, 0, 0, 3, 0, 3),
        (3, 0, 0, 1, 0, 3), (2, 0, 1, 1), (5, 1), (3, 0, 0, 2, 0, 1), (2, 0, 0, 3), (3, 0, 1, 0, 0, 3),
        (3, 0, 1, 2, 0, 3), (2, 0, 1, 2), (3, 0, 1, 2, 0, 1), (4, 0, 0, 0), (4, 0, 1, 3), (2, 0, 1, 3),
        (3, 0, 0, 1, 0, 1), (2, 0, 0, 2), (3, 0, 1, 0, 0, 1), (4, 0, 0, 3), (3, 0, 1, 1, 1, 3), (3, 0, 0, 1, 1, 3),
        (5, 2), (12, 0), (3, 0, 0, 1, 1, 1), (5, 3), (0, 1, 0), (4, 0, 1, 0), (0, 1, 1), (3, 0, 1, 1, 0, 3),
        (6, 0, 0), (3, 0, 1, 2, 1, 1), (3, 0, 0, 2, 0, 3), (3, 1, 0, 0, 0, 1), (3, 0, 1, 2, 1, 3), (7,),
        (3, 0, 1, 1, 1, 1), (3, 0, 0, 2, 1, 3), (1, 1, 0, 1), (6, 2, 0), (1, 1, 1, 3), (1, 1, 1, 1),
        (3, 0, 0, 2, 1, 1), (6, 0, 1), (6, 1, 0), (1, 1, 0, 3), (2, 1, 1, 0), (6, 2, 1), (3, 1, 1, 0, 0, 3),
        (2, 1, 0, 0), (6, 1, 1), (3, 1, 0, 1, 0, 1), (6, 3, 0), (3, 1, 1, 3, 0, 3), (1, 1, 1, 2), (6, 3, 1),
        (3, 1, 0, 0, 0, 3), (3, 1, 0, 3, 0, 1), (2, 1, 1, 3), (3, 1, 0, 3, 0, 3), (8,), (3, 1, 0, 1, 0, 3),
        (2, 1, 1, 1), (9, 0), (9, 1), (3, 1, 0, 0, 1, 1), (3, 1, 0, 0, 1, 3), (1, 1, 0, 2), (2, 1, 0, 1), (9, 2),
        (9, 3), (9, 4), (2, 1, 1, 2), (10, 0), (4, 1, 0, 1), (2, 1, 0, 2), (3, 1, 1, 2, 0, 3), (3, 1, 1, 1, 0, 1),
        (3, 1, 1, 3, 0, 1), (10, 1), (3, 1, 1, 2, 0, 1), (3, 1, 0, 2, 0, 1), (12, 1), (4, 1, 0, 3), (4, 1, 1, 3),
        (3, 1, 0, 2, 1, 1), (3, 1, 1, 1, 1, 3), (3, 1, 1, 1, 0, 3), (3, 1, 0, 2, 0, 3), (11, 0), (3, 1, 1, 0, 0, 1),
        (3, 1, 1, 1, 1, 1), (3, 1, 0, 2, 1, 3), (2, 1, 0, 3), (3, 1, 1, 2, 1, 3), (3, 1, 1, 2, 1, 1), (11, 1),
        (10, 2), (10, 3), (4, 1, 1, 0), (10, 4), (10, 5), (10, 6), (10, 7), (11, 3), (11, 2), (11, 4), (11, 5),
        (11, 6), (11, 7),
    ),
    (
        (0, 0, 1), (0, 0, 0), (1, 0, 0, 3), (1, 0, 1, 1), (1, 0, 0, 1), (3, 0, 0, 0, 0, 1), (1, 0, 1, 3),
        (3, 0, 1, 0, 0, 3), (0, 1, 1), (1, 0, 0, 2), (5, 0), (3, 0, 1, 3, 0, 1), (3, 0, 0, 0, 0, 3), (2, 0, 1, 1),
        (2, 0, 0, 1), (3, 0, 0, 3, 0, 3), (0, 1, 0), (3, 0, 0, 2, 0, 1), (1, 0, 1, 2), (4, 0, 0, 0),
        (3, 0, 0, 3, 0, 1), (2, 0, 0, 0), (3, 0, 1, 0, 0, 1), (2, 0, 0, 2), (2, 0, 1, 0), (3, 0, 1, 3, 0, 3),
        (3, 1, 0, 0, 0, 1), (1, 1, 0, 1), (4, 0, 0, 3), (2, 1, 0, 0), (2, 0, 0, 3), (3, 0, 1, 1, 1, 1),
        (3, 0, 1, 1, 0, 1), (1, 1, 1, 3), (2, 0, 1, 2), (2, 0, 1, 3), (3, 0, 1, 2, 0, 1), (3, 0, 1, 1, 0, 3), (5, 1),
        (3, 0, 0, 1, 0, 3), (3, 0, 0, 2, 0, 3), (3, 0, 0, 1, 0, 1), (6, 0, 0), (3, 0, 0, 1, 1, 3),
        (3, 0, 0, 1, 1, 1), (3, 0, 0, 2, 1, 1), (4, 0, 1, 3), (6, 0, 1), (3, 0, 0, 2, 1, 3), (4, 0, 1, 0),
        (1, 1, 0, 3), (3, 1, 0, 0, 1, 3), (3, 1, 1, 3, 0, 1), (3, 0, 1, 2, 0, 3), (3, 0, 1, 2, 1, 3), (1, 1, 1, 1),
        (3, 0, 1, 1, 1, 3), (5, 2), (3, 1, 1, 0, 0, 1), (3, 1, 1, 3, 0, 3), (6, 2, 0), (3, 0, 1, 2, 1, 1),
        (3, 1, 0, 1, 0, 1), (2, 1, 1, 3), (3, 1, 0, 0, 0, 3), (3, 1, 0, 0, 1, 1), (5, 3), (7,), (3, 1, 1, 0, 0, 3),
        (2, 1, 0, 1), (6, 2, 1), (6, 1, 0), (2, 1, 1, 0), (3, 1, 0, 1, 0, 3), (6, 3, 0), (6, 1, 1), (1, 1, 1, 2),
        (6, 3, 1), (8,), (2, 1, 1, 1), (1, 1, 0, 2), (9, 0), (9, 1), (2, 1, 1, 2), (9, 2), (9, 3), (9, 4), (10, 0),
        (3, 1, 1, 1, 0, 1), (3, 1, 0, 3, 0, 3), (3, 1, 1, 1, 1, 3), (3, 1, 1, 1, 1, 1), (3, 1, 0, 2, 0, 1),
        (3, 1, 1, 1, 0, 3), (3, 1, 0, 3, 0, 1), (3, 1, 1, 2, 0, 1), (4, 1, 0, 1), (2, 1, 0, 3), (3, 1, 0, 2, 0, 3),
        (2, 1, 0, 2), (3, 1, 1, 2, 0, 3), (3, 1, 1, 2, 1, 1), (10, 1), (4, 1, 0, 3), (4, 1, 1, 3), (4, 1, 1, 0),
        (10, 2), (3, 1, 1, 2, 1, 3), (10, 3), (11, 1), (3, 1, 0, 2, 1, 3), (10, 4), (11, 0), (10, 5),
        (3, 1, 0, 2, 1, 1), (11, 2), (10, 6), (10, 7), (11, 4), (11, 5), (11, 6), (11, 3), (11, 7),
    ),
)


def needs_and_sends(event):
    kind, w, cls = event[:3]
    if kind == START:
        own = (w, cls, 0, 0, 0, None)
        return [], [(own, 0, 1), (own, 0, -1), (own, 2, 0), (own, 1, 1), (own, 1, -1)]
    fo = event[3]
    if kind == SPREAD:
        whole = (w, cls, 0, fo, 0, None)
        needs = [whole] if fo != 2 else [whole[:5] + (0,), whole[:5] + (1,)]
        sends = []
        if fo == 3:
            sends.append((whole[:5] + (0,), 0, 1))
        if fo == 1:
            sends.append((whole[:5] + (1,), 0, -1))
        return needs, sends + [(whole, 2, 0), (whole, 1, 1), (whole, 1, -1)]
    if kind == CROSS:
        whole = (w, cls, 1, fo, 0, None)
        return [whole], [(whole, 1, 1), (whole, 1, -1)]
    if kind == RELAY:
        who, go = event[4:]
        whole = (w, cls, who, fo, go, None)
        return [whole], [(whole[:5] + (0 if go == 3 else 1,), 1, 1 if go == 3 else -1)]
    whole = (w, cls, 0, fo, 2, None)
    return [whole[:5] + (0,), whole[:5] + (1,)], [(whole, 2, 0)]


def landing(piece, link, step):
    w, cls, who, fo, go, h = piece
    if link == 0:
        return (w, cls, who, (fo - step) % RING, go, h)
    if link == 1:
        return (w, cls, who, fo, (go - step) % RING, h)
    return (w, cls, 1 - who, fo, go, h)


def in_slab(piece, offset):
    return (piece[3] if piece[1] == 0 else piece[4]) == offset


def layer_kernel(
    quarter, tok, docs, gain, wq, wot, wk, wv, out,
    full_q, full_o, kv_w, hidden, scaled, level, factor, acc_q, acc_kv, query, kv_made, kv, attended, bias, part, part_in,
    w_recv, w_send, own_sem, swap_send, kvw_sem, kv_sem, kv_send, h_sem, h_send, p_recv, p_send, n_send, gate,
):
    section = lax.axis_index("section")
    dp = lax.axis_index("dp")
    tensor = lax.axis_index("tensor")
    z, y, far = dp // 8, (dp // 2) % RING, dp % 2
    group_rows, width = tok.shape[1:]
    rows = 2 * group_rows
    seq = 2 * rows
    block, q_width = wq.shape
    half = block // 2
    small = half // 32 * 16
    chunk = width // PARTS
    slab = 2 * chunk
    kv_width = wk.shape[1]
    weights = (full_q, full_o)
    shards = (wq, wot)

    z_of = [lax.rem(z + d, RING) * 8 for d in range(RING)]
    y_of = [lax.rem(y + d, RING) * 2 for d in range(RING)]
    whose_of = [far, 1 - far]
    z_row, y_row, x_row = ([dp_part * block for dp_part in parts] for parts in (z_of, y_of, whose_of))

    def at(dz, dy):
        return (section, z_of[dz % RING] + y_of[dy % RING] + far, tensor)

    opposite = (section, z_of[0] + y_of[0] + (1 - far), 1 - tensor)
    partner = (section, dp, 1 - tensor)
    core = (1 - section, dp, tensor)
    partner_core = (1 - section, dp, 1 - tensor)
    peers = [at(1, 0), at(-1, 0), at(0, 1), at(0, -1), opposite, partner, core, partner_core]
    barrier = pltpu.get_barrier_semaphore()
    for peer in peers:
        pl.semaphore_signal(barrier, inc=1, device_id=peer, device_id_type=MESH)

    def place(piece):
        w, cls, who, fo, go, h = piece
        dz, dy = (fo, go) if cls == 0 else (go, fo)
        first = z_row[dz] + y_row[dy] + x_row[who] + cls * half
        large = half - small
        cut = large if who == 0 else small
        size = half
        if h == 0:
            size = cut
        if h == 1:
            first, size = first + cut, half - cut
        return weights[w].at[pl.ds(pl.multiple_of(first, 16), size), :]

    def number(piece):
        w, cls, who, fo, go, h = piece
        return w, cls, who, fo * RING + go, 1 if h == 1 else 0

    def copy_of(piece, link, step):
        name = landing(piece, link, step)
        if link == 2:
            target = opposite
        else:
            target = at(step, 0) if link == piece[1] else at(0, step)
        return pltpu.make_async_remote_copy(
            src_ref=place(piece), dst_ref=place(piece), send_sem=w_send.at[number(name)],
            recv_sem=w_recv.at[number(name)], device_id=target, device_id_type=MESH,
        )

    def await_piece(piece):
        ref = place(piece)
        pltpu.make_async_copy(ref, ref, w_recv.at[number(piece)]).wait()

    def own_copy(w, cls):
        return pltpu.make_async_copy(
            shards[w].at[pl.ds(cls * half, half), :], place((w, cls, 0, 0, 0, None)), own_sem.at[w, cls]
        )

    def swap_copy(w, cls):
        return pltpu.make_async_remote_copy(
            src_ref=shards[w].at[pl.ds(cls * half, half), :], dst_ref=place((w, cls, 0, 0, 0, None)),
            send_sem=swap_send.at[w, cls], recv_sem=own_sem.at[w, cls], device_id=partner, device_id_type=MESH,
        )

    def signal_core():
        @pl.when(section == 0)
        def _():
            pl.semaphore_signal(gate, inc=1, device_id=core, device_id_type=MESH)

    def run(event):
        needs, sends = needs_and_sends(event)
        if event[0] == START:
            own_copy(*event[1:]).wait()
        for piece in needs:
            await_piece(piece)
        for send in sends:
            copy_of(*send).start()

    events = [step for step in PROGRAMS[0] if step[0] < UNIT]
    all_sends = [send for event in events for send in needs_and_sends(event)[1]]
    awaited = {piece for event in events for piece in needs_and_sends(event)[0]}

    def rest_of(w, offset):
        for send in all_sends:
            name = landing(*send)
            if name[0] == w and name not in awaited and in_slab(name, offset):
                await_piece(name)

    def cols_of(k):
        first = ((z + ORDER[k // 2]) % RING) * slab + (k % 2) * chunk
        return pl.ds(pl.multiple_of(first, 128), chunk)

    def slab_of(j):
        return pl.ds(pl.multiple_of(((z + ORDER[j]) % RING) * slab, 128), slab)

    kvw_copies = [
        pltpu.make_async_copy(wk, kv_w.at[0], kvw_sem.at[0]),
        pltpu.make_async_copy(wv, kv_w.at[1], kvw_sem.at[1]),
    ]

    def token_copy(k):
        return pltpu.make_async_copy(
            tok.at[:, :, cols_of(k)], hidden.at[:, tensor, :, cols_of(k)], h_sem.at[0, k]
        )

    def token_send(k):
        return pltpu.make_async_remote_copy(
            src_ref=tok.at[:, :, cols_of(k)], dst_ref=hidden.at[:, tensor, :, cols_of(k)],
            send_sem=h_send.at[k], recv_sem=h_sem.at[1, k], device_id=partner, device_id_type=MESH,
        )

    def swap(w):
        @pl.when(far == 1)
        def _():
            for cls in (0, 1):
                swap_copy(w, cls).start()

    @pl.when(far == 0)
    def _():
        for w in (0, 1):
            for cls in (0, 1):
                own_copy(w, cls).start()

    pl.semaphore_wait(barrier, len(peers))

    @pl.when(section == 0)
    def _():
        swap(0)
        for k in range(PARTS):
            token_copy(k).start()
            token_send(k).start()
        swap(1)

    for copy in kvw_copies:
        copy.start()

    def settle():
        for copy in kvw_copies:
            copy.wait()

        def position(index):
            upper = jnp.where(index >= rows, 1, 0)
            odd = jnp.where(index - rows * upper >= group_rows, 1, 0)
            inner = index - rows * upper - group_rows * odd
            segment = sum(jnp.where(inner >= quarter * n, 1, 0) for n in range(1, group_rows // quarter))
            return rows * upper + quarter * odd + inner + segment * quarter

        here = position(lax.broadcasted_iota(jnp.int32, (seq, seq), 1))
        pick = jnp.where(lax.broadcasted_iota(jnp.int32, (seq, seq), 0) == here, 1.0, 0.0)
        along = jnp.broadcast_to(docs[...].astype(jnp.float32), (8, seq))
        docs_row = jnp.dot(along, pick, preferred_element_type=jnp.float32)[:1, :]
        there = position(lax.broadcasted_iota(jnp.int32, (seq, seq), 0))
        pick = lax.broadcasted_iota(jnp.int32, (seq, seq), 1) == there
        docs_col = jnp.sum(jnp.where(pick, docs[...].astype(jnp.float32), 0.0), axis=-1, keepdims=True)
        bias[...] = jnp.where((here <= there) & (docs_row == docs_col), 0.0, -1e30)

    step_rows = 32

    def prepare(j):
        for k in (2 * j, 2 * j + 1):
            for source, whose in ((0, tensor), (1, 1 - tensor)):
                ref = hidden.at[:, whose, :, cols_of(k)]
                pltpu.make_async_copy(ref, ref, h_sem.at[source, k]).wait()

        cols = slab_of(j)
        for n in range(4):

            def body(i, carry):
                there = pl.ds(pl.multiple_of(i * step_rows, step_rows), step_rows)
                here = pl.ds(pl.multiple_of(n * group_rows + i * step_rows, step_rows), step_rows)
                wide = hidden[n // 2, n % 2, there, cols].astype(jnp.float32)
                scaled[j, here, :] = (wide * gain[:, cols]).astype(jnp.bfloat16)
                squares = wide * wide
                total = sum(squares[:, lane : lane + 128] for lane in range(0, slab, 128))
                level[here, :] = total if j == 0 else level[here, :] + total
                return carry

            lax.fori_loop(0, group_rows // step_rows, body, 0)
        for i in (0, 1):
            cols_i = pl.ds(i * kv_width, kv_width)
            term = jnp.dot(scaled[j], kv_w[i, slab_of(j), :], preferred_element_type=jnp.float32)
            acc_kv[:, cols_i] = term if j == 0 else acc_kv[:, cols_i] + term

    tile = 256

    def project(j, share):
        if share == 0:
            rest_of(0, ORDER[j])
        for i in ((0, 1, 2), range(3, q_width // tile))[share]:
            cols = slice(i * tile, (i + 1) * tile)
            term = jnp.dot(scaled[j], full_q[slab_of(j), cols], preferred_element_type=jnp.float32)
            acc_q[:, cols] = term if j == 0 else acc_q[:, cols] + term

    def kv_exchange(i):
        return pltpu.make_async_remote_copy(
            src_ref=kv_made.at[i], dst_ref=kv.at[i], send_sem=kv_send.at[i], recv_sem=kv_sem.at[i],
            device_id=partner, device_id_type=MESH,
        )

    def kv_keep(i):
        return pltpu.make_async_copy(kv_made.at[i], kv.at[i], kv_sem.at[i])

    def finish_kv():
        made = lax.rsqrt(jnp.sum(level[...], axis=-1, keepdims=True) / width + 1e-06)
        factor[...] = made
        for i in (0, 1):
            kv_made[i] = (acc_kv[:, i * kv_width : (i + 1) * kv_width] * made).astype(jnp.bfloat16)

            @pl.when(far == 1)
            def _():
                kv_exchange(i).start()

            @pl.when(far == 0)
            def _():
                kv_keep(i).start()

    def finish_q():
        for i in range(q_width // tile):
            query[:, i * tile : (i + 1) * tile] = (acc_q[:, i * tile : (i + 1) * tile] * factor[...]).astype(jnp.bfloat16)

    scale = 1.0 / HEAD**0.5
    heads = q_width // HEAD
    group = heads // (kv_width // HEAD)

    def attend(pair):
        if pair == 0:
            for i in (0, 1):
                kv_keep(i).wait()
        tasks = [(h, first) for h in (2 * pair, 2 * pair + 1) for first in (0, rows)]
        scores = [
            lax.dot_general(
                query[first : first + rows, h * HEAD : (h + 1) * HEAD],
                kv[0, : first + rows, h // group * HEAD : (h // group + 1) * HEAD],
                (((1,), (1,)), ((), ())),
                preferred_element_type=jnp.float32,
            )
            for h, first in tasks
        ]
        scores = [
            block * scale + bias[first : first + rows, : first + rows] for block, (_, first) in zip(scores, tasks)
        ]
        scores = [jnp.exp(block - jnp.max(block, axis=-1, keepdims=True)) for block in scores]
        mixes = [(block / jnp.sum(block, axis=-1, keepdims=True)).astype(jnp.bfloat16) for block in scores]
        for mix, (h, first) in zip(mixes, tasks):
            attended[first : first + rows, h * HEAD : (h + 1) * HEAD] = jnp.dot(
                mix,
                kv[1, : first + rows, h // group * HEAD : (h // group + 1) * HEAD],
                preferred_element_type=jnp.float32,
            ).astype(jnp.bfloat16)

    def part_send(k):
        return pltpu.make_async_remote_copy(
            src_ref=part.at[k, :, 1 - tensor], dst_ref=part_in.at[k],
            send_sem=p_send.at[k], recv_sem=p_recv.at[k], device_id=partner, device_id_type=MESH,
        )

    def next_send(k, side):
        return pltpu.make_async_remote_copy(
            src_ref=out.at[:, :, cols_of(k)], dst_ref=hidden.at[:, tensor, :, cols_of(k)],
            send_sem=n_send.at[side, k], recv_sem=h_sem.at[side, k],
            device_id=(core, partner_core)[side], device_id_type=MESH,
        )

    def finish(k):
        part_send(k).wait_recv()
        update = part[k, :, tensor].astype(jnp.float32) + part_in[k].astype(jnp.float32)
        own = hidden[:, tensor, :, cols_of(k)].astype(jnp.float32)
        out[:, :, cols_of(k)] = (own + update).astype(jnp.bfloat16)
        if emitted[0] == 0:
            next_send(k, 0).start()
            next_send(k, 1).start()

    def multiply(k):
        if k % 2 == 0:
            rest_of(1, ORDER[k // 2])
        result = lax.dot_general(
            attended[...], full_o[cols_of(k), :], (((1,), (1,)), ((), ())), preferred_element_type=jnp.float32
        )
        part[k] = result.astype(jnp.bfloat16).reshape(part.shape[1:])
        part_send(k).start()

    units = (prepare, project, finish_kv, finish_q, attend, multiply, finish)

    emitted = [0]

    def program(steps, which):
        emitted[0] = which
        for step in steps:
            if step[0] < UNIT:
                run(step)
                continue
            if step[0] == SIGNAL:
                signal_core()
            elif step[0] == AWAIT:
                pl.semaphore_wait(gate, 1)
            else:
                if step == (UNIT, 0) and which == 0:
                    settle()
                units[step[0] - UNIT](*step[1:])

    @pl.when(section == 0)
    def _():
        program(PROGRAMS[0], 0)

    @pl.when(section == 1)
    def _():
        settle()
        pl.semaphore_wait(gate, 1)
        for w in (0, 1):
            swap(w)
        pl.semaphore_wait(gate, 1)
        program(PROGRAMS[1], 1)

    for send in all_sends:
        copy_of(*send).wait_send()
    @pl.when(far == 1)
    def _():
        for w in (0, 1):
            for cls in (0, 1):
                swap_copy(w, cls).wait_send()
        for i in (0, 1):
            kv_exchange(i).wait_send()

    for k in range(PARTS):
        part_send(k).wait_send()

    @pl.when(section == 0)
    def _():
        for k in range(PARTS):
            token_send(k).wait_send()
            next_send(k, 0).wait_send()
            next_send(k, 1).wait_send()


def on_device(tokens, doc_ids, norm_gain, w_query, w_key, w_value, w_out):
    n_segments, quarter, width = tokens.shape[1:]
    rows = n_segments * quarter
    seq = 2 * rows
    block, q_width = w_query.shape[1:]
    kv_width = w_key.shape[2]
    chunk = width // PARTS
    bf16, f32 = jnp.bfloat16, jnp.float32
    dma = pltpu.SemaphoreType.DMA
    anywhere = pl.BlockSpec(memory_space=pl.ANY)
    vmem = pl.BlockSpec(memory_space=pltpu.VMEM)
    state = pl.pallas_call(
        functools.partial(layer_kernel, quarter),
        out_shape=pltpu.VMEM((2, rows // 2, width), bf16),
        in_specs=[anywhere, vmem, vmem] + [anywhere] * 4,
        out_specs=vmem,
        scratch_shapes=[
            pltpu.VMEM((width, q_width), bf16),
            pltpu.VMEM((width, q_width), bf16),
            pltpu.VMEM((2, width, kv_width), bf16),
            pltpu.VMEM((2, 2, rows // 2, width), bf16),
            pltpu.VMEM((RING, seq, 2 * chunk), bf16),
            pltpu.VMEM((seq, 128), f32),
            pltpu.VMEM((seq, 1), f32),
            pltpu.VMEM((seq, q_width), f32),
            pltpu.VMEM((seq, 2 * kv_width), f32),
            pltpu.VMEM((seq, q_width), bf16),
            pltpu.VMEM((2, seq, kv_width), bf16),
            pltpu.VMEM((2, seq, kv_width), bf16),
            pltpu.VMEM((seq, q_width), bf16),
            pltpu.VMEM((seq, seq), f32),
            pltpu.VMEM((PARTS, 2, 2, rows // 2, chunk), bf16),
            pltpu.VMEM((PARTS, 2, rows // 2, chunk), bf16),
            dma((2, 2, 2, RING * RING, 2)),
            dma((2, 2, 2, RING * RING, 2)),
            dma((2, 2)),
            dma((2, 2)),
            dma((2,)),
            dma((2,)),
            dma((2,)),
            dma((2, PARTS)),
            dma((PARTS,)),
            dma((PARTS,)),
            dma((PARTS,)),
            dma((2, PARTS)),
            pltpu.SemaphoreType.REGULAR,
        ],
        compiler_params=pltpu.CompilerParams(
            collective_id=0, has_side_effects=True, vmem_limit_bytes=60 * 1024 * 1024
        ),
        name="layers",
    )(
        tokens[0].reshape(2, rows // 2, width),
        doc_ids,
        norm_gain,
        w_query[0],
        w_out[0].T,
        w_key[0],
        w_value[0],
    )
    return state.reshape(1, 1, n_segments, quarter, width)


def solution(mesh):
    in_specs = (
        P("dp", None, "tensor", None),
        P("dp", None),
        P("section", None),
        P("section", "dp", "tensor"),
        P("section", None, "tensor"),
        P("section", None, "tensor"),
        P("section", "tensor", "dp"),
    )
    out_specs = P("section", "dp", None, "tensor", None)
    return jax.shard_map(
        on_device, mesh=mesh, in_specs=in_specs, out_specs=out_specs, check_vma=False
    )
```

```python
import functools

import jax
import jax.numpy as jnp
from jax import lax
from jax.experimental import pallas as pl
from jax.experimental.pallas import tpu as pltpu
from jax.sharding import PartitionSpec as P

HEAD = 128
MESH = pl.DeviceIdType.MESH
RING = 4
PARTS = 8
ORDER = (0, 1, 3, 2)

START, SPREAD, CROSS, RELAY, LAST, UNIT = range(6)
SIGNAL, AWAIT = 12, 13
PROGRAMS = (
    (
        (0, 0, 0), (0, 0, 1), (1, 0, 0, 3), (1, 0, 1, 1), (1, 0, 1, 3), (1, 0, 0, 1), (2, 0, 1, 0),
        (3, 0, 0, 0, 0, 1), (3, 0, 0, 3, 0, 1), (2, 0, 0, 0), (1, 0, 1, 2), (5, 0), (3, 0, 1, 3, 0, 1),
        (3, 0, 0, 0, 0, 3), (3, 0, 1, 1, 0, 1), (3, 0, 1, 3, 0, 3), (1, 0, 0, 2), (2, 0, 0, 1), (3, 0, 0, 3, 0, 3),
        (3, 0, 0, 1, 0, 3), (2, 0, 1, 1), (5, 1), (3, 0, 0, 2, 0, 1), (2, 0, 0, 3), (3, 0, 1, 0, 0, 3),
        (3, 0, 1, 2, 0, 3), (2, 0, 1, 2), (3, 0, 1, 2, 0, 1), (4, 0, 0, 0), (4, 0, 1, 3), (2, 0, 1, 3),
        (3, 0, 0, 1, 0, 1), (2, 0, 0, 2), (3, 0, 1, 0, 0, 1), (4, 0, 0, 3), (3, 0, 1, 1, 1, 3), (3, 0, 0, 1, 1, 3),
        (5, 2), (12, 0), (3, 0, 0, 1, 1, 1), (5, 3), (0, 1, 0), (4, 0, 1, 0), (0, 1, 1), (3, 0, 1, 1, 0, 3),
        (6, 0, 0), (3, 0, 1, 2, 1, 1), (3, 0, 0, 2, 0, 3), (3, 1, 0, 0, 0, 1), (3, 0, 1, 2, 1, 3), (7,),
        (3, 0, 1, 1, 1, 1), (3, 0, 0, 2, 1, 3), (1, 1, 0, 1), (6, 2, 0), (1, 1, 1, 3), (1, 1, 1, 1),
        (3, 0, 0, 2, 1, 1), (6, 0, 1), (6, 1, 0), (1, 1, 0, 3), (2, 1, 1, 0), (6, 2, 1), (3, 1, 1, 0, 0, 3),
        (2, 1, 0, 0), (6, 1, 1), (3, 1, 0, 1, 0, 1), (6, 3, 0), (3, 1, 1, 3, 0, 3), (1, 1, 1, 2), (6, 3, 1),
        (3, 1, 0, 0, 0, 3), (3, 1, 0, 3, 0, 1), (2, 1, 1, 3), (3, 1, 0, 3, 0, 3), (8,), (3, 1, 0, 1, 0, 3),
        (2, 1, 1, 1), (9, 0), (9, 1), (3, 1, 0, 0, 1, 1), (3, 1, 0, 0, 1, 3), (1, 1, 0, 2), (2, 1, 0, 1), (9, 2),
        (9, 3), (9, 4), (2, 1, 1, 2), (10, 0), (4, 1, 0, 1), (2, 1, 0, 2), (3, 1, 1, 2, 0, 3), (3, 1, 1, 1, 0, 1),
        (3, 1, 1, 3, 0, 1), (10, 1), (3, 1, 1, 2, 0, 1), (3, 1, 0, 2, 0, 1), (12, 1), (12, 2), (12, 3), (12, 4),
        (12, 5), (4, 1, 0, 3), (4, 1, 1, 3), (3, 1, 0, 2, 1, 1), (3, 1, 1, 1, 1, 3), (3, 1, 1, 1, 0, 3),
        (3, 1, 0, 2, 0, 3), (11, 0), (3, 1, 1, 0, 0, 1), (3, 1, 1, 1, 1, 1), (3, 1, 0, 2, 1, 3), (3, 1, 1, 0, 1, 1),
        (3, 1, 1, 0, 1, 3), (2, 1, 0, 3), (3, 1, 1, 2, 1, 3), (3, 1, 1, 2, 1, 1), (11, 1), (10, 2), (10, 3), (10, 4),
        (10, 5), (10, 6), (10, 7), (11, 3), (11, 2), (11, 4), (11, 5), (11, 6), (11, 7),
    ),
    (
        (0, 0, 1), (0, 0, 0), (13, 2), (1, 0, 0, 3), (1, 0, 1, 1), (1, 0, 0, 1), (3, 0, 0, 0, 0, 1), (1, 0, 1, 3),
        (13, 3), (3, 0, 1, 0, 0, 3), (0, 1, 1), (1, 0, 0, 2), (5, 0), (3, 0, 1, 3, 0, 1), (13, 4),
        (3, 0, 0, 0, 0, 3), (2, 0, 1, 1), (2, 0, 0, 1), (3, 0, 0, 3, 0, 3), (0, 1, 0), (13, 5), (3, 0, 0, 2, 0, 1),
        (1, 0, 1, 2), (4, 0, 0, 0), (3, 0, 0, 3, 0, 1), (2, 0, 0, 0), (3, 0, 1, 0, 0, 1), (2, 0, 0, 2), (2, 0, 1, 0),
        (3, 0, 1, 3, 0, 3), (3, 1, 0, 0, 0, 1), (1, 1, 0, 1), (4, 0, 0, 3), (2, 1, 0, 0), (2, 0, 0, 3),
        (3, 0, 1, 1, 1, 1), (3, 0, 1, 1, 0, 1), (1, 1, 1, 3), (2, 0, 1, 2), (2, 0, 1, 3), (3, 0, 1, 2, 0, 1),
        (3, 0, 1, 1, 0, 3), (5, 1), (3, 0, 0, 1, 0, 3), (3, 0, 0, 2, 0, 3), (3, 0, 0, 1, 0, 1), (6, 0, 0),
        (3, 0, 0, 1, 1, 3), (3, 0, 0, 1, 1, 1), (3, 0, 0, 2, 1, 1), (4, 0, 1, 3), (6, 0, 1), (3, 0, 0, 2, 1, 3),
        (4, 0, 1, 0), (1, 1, 0, 3), (3, 1, 0, 0, 1, 3), (3, 1, 1, 3, 0, 1), (3, 0, 1, 2, 0, 3), (3, 0, 1, 2, 1, 3),
        (1, 1, 1, 1), (3, 0, 1, 1, 1, 3), (5, 2), (3, 1, 1, 0, 0, 1), (3, 1, 1, 3, 0, 3), (6, 2, 0),
        (3, 0, 1, 2, 1, 1), (3, 1, 0, 1, 0, 1), (2, 1, 1, 3), (3, 1, 0, 0, 0, 3), (3, 1, 0, 0, 1, 1), (5, 3), (7,),
        (3, 1, 1, 0, 0, 3), (2, 1, 0, 1), (6, 2, 1), (6, 1, 0), (2, 1, 1, 0), (3, 1, 0, 1, 0, 3), (6, 3, 0),
        (6, 1, 1), (1, 1, 1, 2), (6, 3, 1), (8,), (2, 1, 1, 1), (1, 1, 0, 2), (9, 0), (9, 1), (2, 1, 1, 2), (9, 2),
        (9, 3), (9, 4), (10, 0), (3, 1, 1, 1, 0, 1), (3, 1, 0, 3, 0, 3), (3, 1, 1, 1, 1, 3), (3, 1, 1, 1, 1, 1),
        (3, 1, 0, 2, 0, 1), (3, 1, 1, 1, 0, 3), (3, 1, 0, 3, 0, 1), (3, 1, 1, 2, 0, 1), (4, 1, 0, 1), (2, 1, 0, 3),
        (3, 1, 0, 2, 0, 3), (3, 1, 1, 0, 1, 1), (3, 1, 1, 0, 1, 3), (2, 1, 0, 2), (3, 1, 1, 2, 0, 3),
        (3, 1, 1, 2, 1, 1), (10, 1), (4, 1, 0, 3), (4, 1, 1, 3), (10, 2), (3, 1, 1, 2, 1, 3), (10, 3), (11, 1),
        (3, 1, 0, 2, 1, 3), (10, 4), (11, 0), (10, 5), (3, 1, 0, 2, 1, 1), (11, 2), (10, 6), (10, 7), (11, 4),
        (11, 5), (11, 6), (11, 3), (11, 7),
    ),
)


def needs_and_sends(event):
    kind, w, cls = event[:3]
    if kind == START:
        own = (w, cls, 0, 0, 0, None)
        return [], [(own, 0, 1), (own, 0, -1), (own, 2, 0), (own, 1, 1), (own, 1, -1)]
    fo = event[3]
    if kind == SPREAD:
        whole = (w, cls, 0, fo, 0, None)
        needs = [whole] if fo != 2 else [whole[:5] + (0,), whole[:5] + (1,)]
        sends = []
        if fo == 3:
            sends.append((whole[:5] + (0,), 0, 1))
        if fo == 1:
            sends.append((whole[:5] + (1,), 0, -1))
        return needs, sends + [(whole, 2, 0), (whole, 1, 1), (whole, 1, -1)]
    if kind == CROSS:
        whole = (w, cls, 1, fo, 0, None)
        return [whole], [(whole, 1, 1), (whole, 1, -1)]
    if kind == RELAY:
        who, go = event[4:]
        whole = (w, cls, who, fo, go, None)
        return [whole], [(whole[:5] + (0 if go == 3 else 1,), 1, 1 if go == 3 else -1)]
    whole = (w, cls, 0, fo, 2, None)
    return [whole[:5] + (0,), whole[:5] + (1,)], [(whole, 2, 0)]


def landing(piece, link, step):
    w, cls, who, fo, go, h = piece
    if link == 0:
        return (w, cls, who, (fo - step) % RING, go, h)
    if link == 1:
        return (w, cls, who, fo, (go - step) % RING, h)
    return (w, cls, 1 - who, fo, go, h)


def in_slab(piece, offset):
    return (piece[3] if piece[1] == 0 else piece[4]) == offset


def layer_kernel(
    quarter, tok, docs, gain, wq, wot, wk, wv, out,
    full_q, full_o, kv_w, hidden, scaled, level, factor, acc_q, acc_kv, query, kv_made, kv, attended, bias, part, part_in,
    w_recv, w_send, own_sem, swap_send, kvw_sem, kv_sem, kv_send, h_sem, h_send, p_recv, p_send, n_send, gate,
):
    section = lax.axis_index("section")
    dp = lax.axis_index("dp")
    tensor = lax.axis_index("tensor")
    z, y, far = dp // 8, (dp // 2) % RING, dp % 2
    group_rows, width = tok.shape[1:]
    rows = 2 * group_rows
    seq = 2 * rows
    block, q_width = wq.shape
    half = block // 2
    small = half // 32 * 16
    chunk = width // PARTS
    slab = 2 * chunk
    kv_width = wk.shape[1]
    weights = (full_q, full_o)
    shards = (wq, wot)

    z_of = [lax.rem(z + d, RING) * 8 for d in range(RING)]
    y_of = [lax.rem(y + d, RING) * 2 for d in range(RING)]
    whose_of = [far, 1 - far]
    z_row, y_row, x_row = ([dp_part * block for dp_part in parts] for parts in (z_of, y_of, whose_of))

    def at(dz, dy):
        return (section, z_of[dz % RING] + y_of[dy % RING] + far, tensor)

    opposite = (section, z_of[0] + y_of[0] + (1 - far), 1 - tensor)
    partner = (section, dp, 1 - tensor)
    core = (1 - section, dp, tensor)
    partner_core = (1 - section, dp, 1 - tensor)
    peers = [at(1, 0), at(-1, 0), at(0, 1), at(0, -1), opposite, partner, core, partner_core]
    barrier = pltpu.get_barrier_semaphore()
    for peer in peers:
        pl.semaphore_signal(barrier, inc=1, device_id=peer, device_id_type=MESH)

    def place(piece):
        w, cls, who, fo, go, h = piece
        dz, dy = (fo, go) if cls == 0 else (go, fo)
        first = z_row[dz] + y_row[dy] + x_row[who] + cls * half
        large = half - small
        cut = large if who == 0 else small
        size = half
        if h == 0:
            size = cut
        if h == 1:
            first, size = first + cut, half - cut
        return weights[w].at[pl.ds(pl.multiple_of(first, 16), size), :]

    def number(piece):
        w, cls, who, fo, go, h = piece
        return w, cls, who, fo * RING + go, 1 if h == 1 else 0

    def copy_of(piece, link, step):
        name = landing(piece, link, step)
        if link == 2:
            target = opposite
        else:
            target = at(step, 0) if link == piece[1] else at(0, step)
        return pltpu.make_async_remote_copy(
            src_ref=place(piece), dst_ref=place(piece), send_sem=w_send.at[number(name)],
            recv_sem=w_recv.at[number(name)], device_id=target, device_id_type=MESH,
        )

    def await_piece(piece):
        ref = place(piece)
        pltpu.make_async_copy(ref, ref, w_recv.at[number(piece)]).wait()

    def own_copy(w, cls):
        return pltpu.make_async_copy(
            shards[w].at[pl.ds(cls * half, half), :], place((w, cls, 0, 0, 0, None)), own_sem.at[w, cls]
        )

    def swap_copy(w, cls):
        return pltpu.make_async_remote_copy(
            src_ref=shards[w].at[pl.ds(cls * half, half), :], dst_ref=place((w, cls, 0, 0, 0, None)),
            send_sem=swap_send.at[w, cls], recv_sem=own_sem.at[w, cls], device_id=partner, device_id_type=MESH,
        )

    def signal_core():
        @pl.when(section == 0)
        def _():
            pl.semaphore_signal(gate, inc=1, device_id=core, device_id_type=MESH)

    def run(event):
        needs, sends = needs_and_sends(event)
        if event[0] == START:
            own_copy(*event[1:]).wait()
        for piece in needs:
            await_piece(piece)
        for send in sends:
            copy_of(*send).start()

    events = [step for step in PROGRAMS[0] if step[0] < UNIT]
    all_sends = [send for event in events for send in needs_and_sends(event)[1]]
    awaited = {piece for event in events for piece in needs_and_sends(event)[0]}

    def rest_of(w, offset):
        for send in all_sends:
            name = landing(*send)
            if name[0] == w and name not in awaited and in_slab(name, offset):
                await_piece(name)

    def cols_of(k):
        first = ((z + ORDER[k // 2]) % RING) * slab + (k % 2) * chunk
        return pl.ds(pl.multiple_of(first, 128), chunk)

    def slab_of(j):
        return pl.ds(pl.multiple_of(((z + ORDER[j]) % RING) * slab, 128), slab)

    kvw_copies = [
        pltpu.make_async_copy(wk, kv_w.at[0], kvw_sem.at[0]),
        pltpu.make_async_copy(wv, kv_w.at[1], kvw_sem.at[1]),
    ]

    def token_copy(k):
        return pltpu.make_async_copy(
            tok.at[:, :, cols_of(k)], hidden.at[:, tensor, :, cols_of(k)], h_sem.at[0, k]
        )

    def token_send(k):
        return pltpu.make_async_remote_copy(
            src_ref=tok.at[:, :, cols_of(k)], dst_ref=hidden.at[:, tensor, :, cols_of(k)],
            send_sem=h_send.at[k], recv_sem=h_sem.at[1, k], device_id=partner, device_id_type=MESH,
        )

    def swap(w):
        @pl.when(far == 1)
        def _():
            for cls in (0, 1):
                swap_copy(w, cls).start()

    @pl.when(far == 0)
    def _():
        for w in (0, 1):
            for cls in (0, 1):
                own_copy(w, cls).start()

    pl.semaphore_wait(barrier, len(peers))

    @pl.when(section == 0)
    def _():
        swap(0)
        for k in range(PARTS):
            token_copy(k).start()
            token_send(k).start()
        swap(1)

    for copy in kvw_copies:
        copy.start()

    def settle():
        for copy in kvw_copies:
            copy.wait()

        def position(index):
            upper = jnp.where(index >= rows, 1, 0)
            odd = jnp.where(index - rows * upper >= group_rows, 1, 0)
            inner = index - rows * upper - group_rows * odd
            segment = sum(jnp.where(inner >= quarter * n, 1, 0) for n in range(1, group_rows // quarter))
            return rows * upper + quarter * odd + inner + segment * quarter

        here = position(lax.broadcasted_iota(jnp.int32, (seq, seq), 1))
        pick = jnp.where(lax.broadcasted_iota(jnp.int32, (seq, seq), 0) == here, 1.0, 0.0)
        along = jnp.broadcast_to(docs[...].astype(jnp.float32), (8, seq))
        docs_row = jnp.dot(along, pick, preferred_element_type=jnp.float32)[:1, :]
        there = position(lax.broadcasted_iota(jnp.int32, (seq, seq), 0))
        pick = lax.broadcasted_iota(jnp.int32, (seq, seq), 1) == there
        docs_col = jnp.sum(jnp.where(pick, docs[...].astype(jnp.float32), 0.0), axis=-1, keepdims=True)
        bias[...] = jnp.where((here <= there) & (docs_row == docs_col), 0.0, -1e30)

    step_rows = 32

    def prepare(j):
        for k in (2 * j, 2 * j + 1):
            for source, whose in ((0, tensor), (1, 1 - tensor)):
                ref = hidden.at[:, whose, :, cols_of(k)]
                pltpu.make_async_copy(ref, ref, h_sem.at[source, k]).wait()

        cols = slab_of(j)
        for n in range(4):

            def body(i, carry):
                there = pl.ds(pl.multiple_of(i * step_rows, step_rows), step_rows)
                here = pl.ds(pl.multiple_of(n * group_rows + i * step_rows, step_rows), step_rows)
                wide = hidden[n // 2, n % 2, there, cols].astype(jnp.float32)
                scaled[j, here, :] = (wide * gain[:, cols]).astype(jnp.bfloat16)
                squares = wide * wide
                total = sum(squares[:, lane : lane + 128] for lane in range(0, slab, 128))
                level[here, :] = total if j == 0 else level[here, :] + total
                return carry

            lax.fori_loop(0, group_rows // step_rows, body, 0)
        for i in (0, 1):
            cols_i = pl.ds(i * kv_width, kv_width)
            term = jnp.dot(scaled[j], kv_w[i, slab_of(j), :], preferred_element_type=jnp.float32)
            acc_kv[:, cols_i] = term if j == 0 else acc_kv[:, cols_i] + term

    tile = 256

    def project(j, share):
        if share == 0:
            rest_of(0, ORDER[j])
        for i in ((0, 1, 2), range(3, q_width // tile))[share]:
            cols = slice(i * tile, (i + 1) * tile)
            term = jnp.dot(scaled[j], full_q[slab_of(j), cols], preferred_element_type=jnp.float32)
            acc_q[:, cols] = term if j == 0 else acc_q[:, cols] + term

    def kv_exchange(i):
        return pltpu.make_async_remote_copy(
            src_ref=kv_made.at[i], dst_ref=kv.at[i], send_sem=kv_send.at[i], recv_sem=kv_sem.at[i],
            device_id=partner, device_id_type=MESH,
        )

    def kv_keep(i):
        return pltpu.make_async_copy(kv_made.at[i], kv.at[i], kv_sem.at[i])

    def finish_kv():
        made = lax.rsqrt(jnp.sum(level[...], axis=-1, keepdims=True) / width + 1e-06)
        factor[...] = made
        for i in (0, 1):
            kv_made[i] = (acc_kv[:, i * kv_width : (i + 1) * kv_width] * made).astype(jnp.bfloat16)

            @pl.when(far == 1)
            def _():
                kv_exchange(i).start()

            @pl.when(far == 0)
            def _():
                kv_keep(i).start()

    def finish_q():
        for i in range(q_width // tile):
            query[:, i * tile : (i + 1) * tile] = (acc_q[:, i * tile : (i + 1) * tile] * factor[...]).astype(jnp.bfloat16)

    scale = 1.0 / HEAD**0.5
    heads = q_width // HEAD
    group = heads // (kv_width // HEAD)

    def attend(pair):
        if pair == 0:
            for i in (0, 1):
                kv_keep(i).wait()
        tasks = [(h, first) for h in (2 * pair, 2 * pair + 1) for first in (0, rows)]
        scores = [
            lax.dot_general(
                query[first : first + rows, h * HEAD : (h + 1) * HEAD],
                kv[0, : first + rows, h // group * HEAD : (h // group + 1) * HEAD],
                (((1,), (1,)), ((), ())),
                preferred_element_type=jnp.float32,
            )
            for h, first in tasks
        ]
        scores = [
            block * scale + bias[first : first + rows, : first + rows] for block, (_, first) in zip(scores, tasks)
        ]
        scores = [jnp.exp(block - jnp.max(block, axis=-1, keepdims=True)) for block in scores]
        mixes = [(block / jnp.sum(block, axis=-1, keepdims=True)).astype(jnp.bfloat16) for block in scores]
        for mix, (h, first) in zip(mixes, tasks):
            attended[first : first + rows, h * HEAD : (h + 1) * HEAD] = jnp.dot(
                mix,
                kv[1, : first + rows, h // group * HEAD : (h // group + 1) * HEAD],
                preferred_element_type=jnp.float32,
            ).astype(jnp.bfloat16)

    def part_send(k):
        return pltpu.make_async_remote_copy(
            src_ref=part.at[k, :, 1 - tensor], dst_ref=part_in.at[k],
            send_sem=p_send.at[k], recv_sem=p_recv.at[k], device_id=partner, device_id_type=MESH,
        )

    def next_send(k, side):
        return pltpu.make_async_remote_copy(
            src_ref=out.at[:, :, cols_of(k)], dst_ref=hidden.at[:, tensor, :, cols_of(k)],
            send_sem=n_send.at[side, k], recv_sem=h_sem.at[side, k],
            device_id=(core, partner_core)[side], device_id_type=MESH,
        )

    def finish(k):
        part_send(k).wait_recv()
        update = part[k, :, tensor].astype(jnp.float32) + part_in[k].astype(jnp.float32)
        own = hidden[:, tensor, :, cols_of(k)].astype(jnp.float32)
        out[:, :, cols_of(k)] = (own + update).astype(jnp.bfloat16)
        if emitted[0] == 0:
            next_send(k, 0).start()
            next_send(k, 1).start()

    def multiply(k):
        if k % 2 == 0:
            rest_of(1, ORDER[k // 2])
        result = lax.dot_general(
            attended[...], full_o[cols_of(k), :], (((1,), (1,)), ((), ())), preferred_element_type=jnp.float32
        )
        part[k] = result.astype(jnp.bfloat16).reshape(part.shape[1:])
        part_send(k).start()

    units = (prepare, project, finish_kv, finish_q, attend, multiply, finish)

    emitted = [0]

    def program(steps, which):
        emitted[0] = which
        for step in steps:
            if step[0] < UNIT:
                run(step)
                continue
            if step[0] == SIGNAL:
                signal_core()
            elif step[0] == AWAIT:
                pl.semaphore_wait(gate, 1)
            else:
                if step == (UNIT, 0) and which == 0:
                    settle()
                units[step[0] - UNIT](*step[1:])

    @pl.when(section == 0)
    def _():
        program(PROGRAMS[0], 0)

    @pl.when(section == 1)
    def _():
        settle()
        pl.semaphore_wait(gate, 1)
        for w in (0, 1):
            swap(w)
        pl.semaphore_wait(gate, 1)
        program(PROGRAMS[1], 1)

    for send in all_sends:
        copy_of(*send).wait_send()
    @pl.when(far == 1)
    def _():
        for w in (0, 1):
            for cls in (0, 1):
                swap_copy(w, cls).wait_send()
        for i in (0, 1):
            kv_exchange(i).wait_send()

    for k in range(PARTS):
        part_send(k).wait_send()

    @pl.when(section == 0)
    def _():
        for k in range(PARTS):
            token_send(k).wait_send()
            next_send(k, 0).wait_send()
            next_send(k, 1).wait_send()


def on_device(tokens, doc_ids, norm_gain, w_query, w_key, w_value, w_out):
    n_segments, quarter, width = tokens.shape[1:]
    rows = n_segments * quarter
    seq = 2 * rows
    block, q_width = w_query.shape[1:]
    kv_width = w_key.shape[2]
    chunk = width // PARTS
    bf16, f32 = jnp.bfloat16, jnp.float32
    dma = pltpu.SemaphoreType.DMA
    anywhere = pl.BlockSpec(memory_space=pl.ANY)
    vmem = pl.BlockSpec(memory_space=pltpu.VMEM)
    state = pl.pallas_call(
        functools.partial(layer_kernel, quarter),
        out_shape=pltpu.VMEM((2, rows // 2, width), bf16),
        in_specs=[anywhere, vmem, vmem] + [anywhere] * 4,
        out_specs=vmem,
        scratch_shapes=[
            pltpu.VMEM((width, q_width), bf16),
            pltpu.VMEM((width, q_width), bf16),
            pltpu.VMEM((2, width, kv_width), bf16),
            pltpu.VMEM((2, 2, rows // 2, width), bf16),
            pltpu.VMEM((RING, seq, 2 * chunk), bf16),
            pltpu.VMEM((seq, 128), f32),
            pltpu.VMEM((seq, 1), f32),
            pltpu.VMEM((seq, q_width), f32),
            pltpu.VMEM((seq, 2 * kv_width), f32),
            pltpu.VMEM((seq, q_width), bf16),
            pltpu.VMEM((2, seq, kv_width), bf16),
            pltpu.VMEM((2, seq, kv_width), bf16),
            pltpu.VMEM((seq, q_width), bf16),
            pltpu.VMEM((seq, seq), f32),
            pltpu.VMEM((PARTS, 2, 2, rows // 2, chunk), bf16),
            pltpu.VMEM((PARTS, 2, rows // 2, chunk), bf16),
            dma((2, 2, 2, RING * RING, 2)),
            dma((2, 2, 2, RING * RING, 2)),
            dma((2, 2)),
            dma((2, 2)),
            dma((2,)),
            dma((2,)),
            dma((2,)),
            dma((2, PARTS)),
            dma((PARTS,)),
            dma((PARTS,)),
            dma((PARTS,)),
            dma((2, PARTS)),
            pltpu.SemaphoreType.REGULAR,
        ],
        compiler_params=pltpu.CompilerParams(
            collective_id=0, has_side_effects=True, vmem_limit_bytes=60 * 1024 * 1024
        ),
        name="layers",
    )(
        tokens[0].reshape(2, rows // 2, width),
        doc_ids,
        norm_gain,
        w_query[0],
        w_out[0].T,
        w_key[0],
        w_value[0],
    )
    return state.reshape(1, 1, n_segments, quarter, width)


def solution(mesh):
    in_specs = (
        P("dp", None, "tensor", None),
        P("dp", None),
        P("section", None),
        P("section", "dp", "tensor"),
        P("section", None, "tensor"),
        P("section", None, "tensor"),
        P("section", "tensor", "dp"),
    )
    out_specs = P("section", "dp", None, "tensor", None)
    return jax.shard_map(
        on_device, mesh=mesh, in_specs=in_specs, out_specs=out_specs, check_vma=False
    )
```
